1024 devices in a mesh: patch: 32 (over y, z_hi, core), det: 32 (over x, z_lo).
Axes of the slice: x: 8, y: 8, z: 8 (z_hi: 2, z_lo: 4; z = z_hi * 4 + z_lo), core: 2. Of those that a mesh axis runs over, the one named last changes fastest.
Arguments:
- tod_image: float32 [32, 32, 128, 1024], P('patch', 'det'), may hold values from -6 to 6
- angles: float32 [32, 32, 128, 1024], P('patch', 'det'), may hold values from -3.140625 to 3.140625
- pixel_offset: int32 [32, 32, 128, 1024], P('patch', 'det'), may hold values from 0 to 63
- target_patch: int32 [32, 32, 128, 1], P('patch', 'det'), may hold values from 0 to 31; in each aligned block of 128 rows (0 to 127, 128 to 255, ..., all dimensions but the last counted through in order) at most 8 rows name the same one
- target_block: int32 [32, 32, 128], P('patch', 'det'), may hold values from 0 to 255
- noise_spectrum: float32 [32, 32, 4, 513], P('patch', 'det'), may hold values from 0.1 to 1
- residual: float32 [32, 256, 3, 64], P('patch', 'det'), may hold values from -6 to 6
- previous_rz: float32 [1], replicated, may hold values from 2097152 to 33554432
- legendre: float32 [128, 64, 64], P('det'), may hold values from -0.75 to 0.75
- harmonic_filter: float32 [128, 64], P('det'), may hold values from 0.53333336 to 10.666667
Outputs:
- new_residual: float32 [32, 256, 3, 64], P('patch', 'det')
- preconditioned: float32 [32, 128, 6, 64], P('patch', 'det')
- beta: float32 [1], replicated
The draws below stay inside these ranges and needn't reach their ends.
Inputs may be any that keep to these rules, and one draw needn't show every extreme that they name: `target_patch`: among the 128 blocks of one device at most 8 name the same patch, a bound that some device reaches.
All inputs are finite; a program needn't handle non-finite values.
Results may differ from the reference program's by a relative error of at most 0.0003.
Values sent between devices are 32-bit elements; how exact they have to be, the bound alone decides.
A program may use at most 32 MiB of HBM per device.

```python
import math
import jax
import jax.numpy as jnp
import numpy as np
from jax import lax

BS = 1024
PIXB = 64
NPHI = 256
SB = 128
DET_DEV = 4
FREQ = 513
BPR = 4
NRING = 64
PBLK = 256
MMAX = 128
NL = 64
CAP = 8
N_PATCH = 32
N_DET = 32


def set_ends(drawn, rng, low, high):
    longest = drawn.shape.index(max(drawn.shape))
    spots = []
    for shift in (0, 1):
        where = [jax.random.randint(jax.random.fold_in(rng, axis), (), 0, length) for axis, length in enumerate(drawn.shape)]
        where[longest] = (where[longest] + shift) % drawn.shape[longest]
        spots.append(tuple(where))
    return drawn.at[spots[0]].set(low).at[spots[1]].set(high)


def block_levels(stream_key, shape, shards, least, top_value):
    loudness, own = 1.0, jax.random.fold_in(stream_key, 6)
    for axis_at, blocks in shards:
        steps = jnp.exp(jax.random.uniform(jax.random.fold_in(own, axis_at), (blocks,), jnp.float32, least / len(shards), top_value / len(shards)))
        loudness = loudness * jnp.repeat(steps, shape[axis_at] // blocks).reshape([-1 if axis == axis_at else 1 for axis in range(len(shape))])
    return loudness


def shared_out(own_key, own, number, rows, number_of, top, limit, slope):
    ranking = jax.random.permutation(own_key, number_of)
    heavy_load, usual = portions_of(number_of, rows * top, limit, slope, True), portions_of(number_of, rows * top, limit, slope, False)
    places = jnp.arange(number_of)

    def named(sizes, turn):
        used = int((sizes > 0).sum())
        fixed = max(1, used // 4)
        passed = fixed + (places - fixed + turn * (used - fixed)) % max(1, number_of - fixed)
        return jnp.zeros((number_of,), jnp.int32).at[ranking[jnp.where(places < fixed, places, passed)]].set(jnp.asarray(sizes, jnp.int32))

    sizes = jnp.where(number % 4 == 0, named(heavy_load, number // 4), named(usual, number - number // 4 - 1))
    mixed = jax.random.permutation(jax.random.fold_in(own, 3), number_of)
    source_of, taker = mixed[0:number_of // 2 * 2:2], mixed[1:number_of // 2 * 2:2]
    slack = jnp.minimum(sizes[source_of] - 1, limit - sizes[taker]) // 2
    slack = jnp.where((source_of == ranking[0]) | (taker == ranking[0]) | (sizes[taker] == 0), 0, jnp.maximum(slack, 0))
    passed = jax.random.randint(jax.random.fold_in(own, 4), (number_of // 2,), 0, 1 << 20) % (slack + 1)
    sizes = sizes.at[source_of].add(-passed).at[taker].add(passed)
    members = jnp.searchsorted(jnp.cumsum(sizes), jnp.arange(rows * top), side="right").astype(jnp.int32)
    listing = members.reshape(top, rows).T
    listing = listing[jax.random.permutation(jax.random.fold_in(own, 1), rows)]
    turn = jax.random.randint(jax.random.fold_in(own, 2), (rows, 1), 0, top)
    return jnp.take_along_axis(listing, (jnp.arange(top)[None, :] + turn) % top, axis=1)


def portions_of(amount, total, most, lean, full):
    weights = [(1 << 20) // math.isqrt(grade ** lean) + 1 for grade in range(1, amount + 1)]
    largest = most if full else min(most, max(-(-total // amount), total * weights[0] // sum(weights)))
    least = 1 if total - largest >= amount - 1 else 0
    given, rest = [largest] + [least] * (amount - 1), total - largest - least * (amount - 1)
    while rest > 0:
        movable = [i for i in range(1, amount) if given[i] < largest] or [i for i in range(1, amount) if given[i] < most]
        mass, remaining = sum([weights[i] for i in movable]), rest
        for i in movable:
            more = min(most - given[i], max(1, remaining * weights[i] // mass), rest)
            given[i] = given[i] + more
            rest = rest - more
    return np.array(given)


def gaussian(key, extent, width, reach, shards=(), dtype=jnp.bfloat16):
    array = width * jax.random.normal(key, extent, jnp.float32)
    if shards:
        array = array * block_levels(key, extent, shards, -0.22, 0.18)
    return jnp.clip(array, -reach, reach).astype(dtype)


def setup_inputs(seed: int = 0) -> dict:
    key_of = jax.random.split(jax.random.key(seed), 11)
    tod_image = gaussian(key_of[0], (N_PATCH, N_DET, SB, BS), 1.0, 6.0, ((0, 32), (1, 32)), jnp.float32)
    angles = jnp.clip(jax.random.uniform(key_of[1], (N_PATCH, N_DET, SB, BS), jnp.float32, -3.140625, 3.140625), -3.140625, 3.140625)
    pixel_offset = set_ends(jax.random.randint(key_of[2], (N_PATCH, N_DET, SB, BS), 0, PIXB), jax.random.fold_in(key_of[2], 1), 0, PIXB - 1).astype(jnp.int32)
    target_patch_keys = jax.random.split(jax.random.fold_in(key_of[3], 1), N_PATCH * N_DET * SB // SB)
    target_patch_turns = jax.random.permutation(jax.random.fold_in(key_of[3], 3), N_PATCH * N_DET * SB // SB)
    target_patch = jax.vmap(lambda own, number: shared_out(jax.random.fold_in(key_of[3], 2), own, number, SB, N_PATCH, 1, CAP, 2))(target_patch_keys, target_patch_turns).reshape((N_PATCH, N_DET, SB, 1))
    target_block = set_ends(jax.random.randint(key_of[4], (N_PATCH, N_DET, SB), 0, PBLK), jax.random.fold_in(key_of[4], 1), 0, PBLK - 1).astype(jnp.int32)
    noise_spectrum = jnp.clip(jnp.exp(math.log(1.0) - 2.3025851 * jax.random.uniform(key_of[5], (N_PATCH, N_DET, DET_DEV, FREQ), jnp.float32) ** block_levels(key_of[5], (N_PATCH, N_DET, DET_DEV, FREQ), ((0, 32), (1, 32)), -0.2, 0.2)), 0.1, 1.0)
    residual = gaussian(key_of[6], (N_PATCH, PBLK, 3, PIXB), 1.0, 6.0, ((0, 32), (1, 32)), jnp.float32)
    previous_rz = jnp.clip(jnp.exp(jax.random.uniform(key_of[7], (1,), jnp.float32, math.log(2097152), math.log(33554432))), 2097152, 33554432)
    legendre = gaussian(key_of[8], (MMAX, NL, NRING), NRING ** -0.5, 0.75, ((0, 32),), jnp.float32)
    harmonic_filter = jnp.clip(jnp.exp(math.log(10.666667) - 2.9957323 * jax.random.uniform(key_of[9], (MMAX, NL), jnp.float32) ** block_levels(key_of[9], (MMAX, NL), ((0, 32),), -0.2, 0.2)), 0.53333336, 10.666667)
    return {"tod_image": tod_image, "angles": angles, "pixel_offset": pixel_offset, "target_patch": target_patch, "target_block": target_block, "noise_spectrum": noise_spectrum, "residual": residual, "previous_rz": previous_rz, "legendre": legendre, "harmonic_filter": harmonic_filter}


def reference(tod_image, angles, pixel_offset, target_patch, target_block, noise_spectrum, residual, previous_rz, legendre, harmonic_filter):
    device_count = N_PATCH * N_DET
    total_pixels = N_PATCH * PBLK * PIXB

    def device_step(carry, inputs):
        image_flat, curvature = carry
        samples, angle_rows, offsets, patch_ids, block_ids, spectrum = inputs
        spectrum_rows = jnp.repeat(spectrum, SB // DET_DEV, axis=0)
        filtered = jnp.fft.irfft(jnp.fft.rfft(samples, axis=1) * spectrum_rows, n=BS, axis=1).astype(jnp.float32)
        curvature = curvature + jnp.sum(samples * filtered)
        weighted = jnp.stack([filtered, filtered * jnp.cos(2.0 * angle_rows), filtered * jnp.sin(2.0 * angle_rows)], axis=-1)
        pixel_ids = ((patch_ids * PBLK + block_ids)[:, None] * PIXB + offsets).astype(jnp.int32)
        image_flat = image_flat.at[pixel_ids.reshape(-1)].add(weighted.reshape(-1, 3))
        return ((image_flat, curvature), None)
    inputs = (tod_image.reshape(device_count, SB, BS), angles.reshape(device_count, SB, BS), pixel_offset.reshape(device_count, SB, BS), target_patch.reshape(device_count, SB), target_block.reshape(device_count, SB), noise_spectrum.reshape(device_count, DET_DEV, FREQ))
    initial = (jnp.zeros((total_pixels, 3), jnp.float32), jnp.zeros((), jnp.float32))
    (image_flat, curvature), unused = lax.scan(device_step, initial, inputs)
    image = image_flat.reshape(N_PATCH, PBLK, PIXB, 3).transpose(0, 1, 3, 2)
    step_size = previous_rz[0] / curvature
    new_residual = residual - step_size * image
    fields = new_residual.reshape(N_PATCH, NRING, BPR, 3, PIXB).transpose(0, 1, 3, 2, 4).reshape(N_PATCH, NRING, 3, NPHI)
    spectrum_all = jnp.fft.rfft(fields, axis=3)[..., :MMAX]
    norm_factor = math.sqrt(2.0 / NPHI)
    cos_part = (jnp.real(spectrum_all) * norm_factor).astype(jnp.float32)
    sin_part = (-jnp.imag(spectrum_all) * norm_factor).astype(jnp.float32)
    columns = jnp.stack([cos_part, sin_part], axis=-1)
    columns = columns.transpose(0, 3, 1, 2, 4).reshape(N_PATCH, MMAX, NRING, 6)
    coefficients = jnp.einsum('mlr,pmrc->pmcl', legendre, columns, precision=lax.Precision.HIGHEST)
    preconditioned = harmonic_filter[None, :, None, :] * coefficients
    rz_after = jnp.sum(preconditioned * coefficients)
    beta = jnp.reshape(rz_after / previous_rz[0], (1,))
    return (new_residual, preconditioned, beta)
```

```python
import functools
import math

import jax
import jax.numpy as jnp
import numpy as np
from jax import lax
from jax.experimental import pallas as pl
from jax.experimental.pallas import tpu as pltpu
from jax.sharding import PartitionSpec as P

BF16 = jnp.bfloat16
F32 = jnp.float32
I32 = jnp.int32
MESH = pl.DeviceIdType.MESH
LANES = 128
RADIX = 8
GROUP = 16
HIGH = 4
LOW = 16
LABEL_LANE = 12
CURVE_LANE = 13
ROOT_HALF = math.sqrt(0.5)


def split2(x):
    hi = x.astype(BF16)
    return hi, (x - hi.astype(F32)).astype(BF16)


def split3(x):
    hi = x.astype(BF16)
    rest = x - hi.astype(F32)
    mid = rest.astype(BF16)
    return hi, mid, (rest - mid.astype(F32)).astype(BF16)


def dot(a, b):
    return lax.dot_general(a, b, (((1,), (0,)), ((), ())), preferred_element_type=F32)


def dot_nt(a, b):
    return lax.dot_general(a, b, (((1,), (1,)), ((), ())), preferred_element_type=F32)


def iota(shape, dim):
    return lax.broadcasted_iota(I32, shape, dim)


def np_split_rows(table):
    hi = table.astype(np.float32).astype(BF16)
    lo = (table - hi.astype(np.float64)).astype(np.float32).astype(BF16)
    return np.concatenate([hi, hi, lo], axis=0)


def fourier_matrix():
    j = np.arange(LANES)
    angle = 2.0 * np.pi * (np.outer(j, j) % LANES) / LANES
    c, s = np.cos(angle), np.sin(angle)
    return np_split_rows(np.block([[c, -s], [s, c]]))


def twiddle_rows():
    n = np.arange(LANES)
    angle = [2.0 * np.pi * n * k / (RADIX * LANES) for k in range(1, 5)]
    return np.stack([np.cos(a) for a in angle] + [np.sin(a) for a in angle]).astype(np.float32)


def cycle_matrix(modes_here):
    f = np.arange(256)[:, None]
    lane = np.arange(LANES)
    mode = (-(lane // modes_here) % (LANES // modes_here)) * modes_here + lane % modes_here
    angle = 2.0 * np.pi * (f * mode % 256) / 256.0
    scale = math.sqrt(2.0 / 256.0)
    return np_split_rows(np.concatenate([np.cos(angle), np.sin(angle)], axis=1) * scale)


def pixel_spread():
    col = np.arange(3 * 256)
    s, pixel = col // 256, col % 64
    a, c = pixel // LOW, pixel % LOW
    source = (c // 8) * LANES + (c % 8) * 16 + s * HIGH + a
    return (np.arange(256)[:, None] == source).astype(np.float32).astype(BF16)


def double_angle(theta):
    n = jnp.round(theta * (2.0 / math.pi))
    odd = (n.astype(I32) & 1) == 1
    hi = np.float32(math.pi / 2)
    lo = np.float32(math.pi / 2 - float(hi))
    r = (theta - n * hi) - n * lo
    y = r * r
    c = jnp.full_like(y, COS_POLY[-1])
    for coef in COS_POLY[-2::-1]:
        c = c * y + coef
    s = jnp.full_like(y, SIN_POLY[-1])
    for coef in SIN_POLY[-2::-1]:
        s = s * y + coef
    return odd, c, s * r


def fit_polys():
    top = (math.pi / 4) ** 2 * 1.0001
    y = top * 0.5 * (1.0 - np.cos(np.pi * (np.arange(400) + 0.5) / 400))
    r = np.sqrt(y)
    power = y[:, None] ** np.arange(6)
    cos_c = np.linalg.lstsq(power, np.cos(2 * r), rcond=None)[0]
    sin_c = np.linalg.lstsq(power[:, :5], np.sin(2 * r) / r, rcond=None)[0]
    return [float(np.float32(v)) for v in cos_c], [float(np.float32(v)) for v in sin_c]


COS_POLY, SIN_POLY = fit_polys()


def filter_blocks(x, spec_ref, table, tw):
    blocks = x.shape[0]
    dets = spec_ref.shape[0]
    t = [x[:, i * LANES : (i + 1) * LANES] for i in range(RADIX)]
    a = [t[i] + t[i + 4] for i in range(4)]
    b = [t[i] - t[i + 4] for i in range(4)]
    even, odd = a[0] + a[2], a[1] + a[3]
    diff, both = (b[1] - b[3]) * ROOT_HALF, (b[1] + b[3]) * ROOT_HALF
    y = [
        (even + odd, None),
        (b[0] + diff, -(b[2] + both)),
        (a[0] - a[2], a[3] - a[1]),
        (b[0] - diff, b[2] - both),
        (even - odd, None),
    ]
    rows = [jnp.concatenate([y[0][0], jnp.zeros_like(x[:, :LANES])], axis=1)]
    for k in range(1, 5):
        c, s = tw[k - 1 : k, :], tw[k + 3 : k + 4, :]
        re, im = y[k]
        if im is None:
            rows.append(jnp.concatenate([re * c, -(re * s)], axis=1))
        else:
            rows.append(jnp.concatenate([re * c + im * s, im * c - re * s], axis=1))
    hi, lo = split2(jnp.concatenate(rows, axis=0))
    spectrum = dot(jnp.concatenate([hi, lo, hi], axis=1), table)

    col = iota((1, 5 * LANES), 1)
    k_of, j_of = col // LANES, col % LANES
    order = k_of + RADIX * j_of
    place = jnp.minimum(order, RADIX * LANES - order)
    pick = (iota((512, 5 * LANES), 0) == place).astype(F32).astype(BF16)
    own = spec_ref[...]
    parts = split3(own[:, :512])
    weight = dot(parts[0], pick) + dot(parts[1], pick) + dot(parts[2], pick)
    weight = weight + jnp.where(place == 512, own[:, 512:513], 0.0)
    edge = (k_of == 0) | (k_of == 4)
    weight = weight * jnp.where(edge, 1.0 / 1024.0, 2.0 / 1024.0)

    per = blocks // dets
    scaled = []
    for k in range(5):
        w = weight[:, k * LANES : (k + 1) * LANES]
        w = jnp.concatenate([w, -w], axis=1)
        for d in range(dets):
            part = spectrum[k * blocks + d * per : k * blocks + (d + 1) * per, :]
            scaled.append(part * w[d : d + 1, :])
    hi, lo = split2(jnp.concatenate(scaled, axis=0))
    u = dot(jnp.concatenate([hi, lo, hi], axis=1), table)
    re = [u[k * blocks : (k + 1) * blocks, :LANES] for k in range(5)]
    im = [u[k * blocks : (k + 1) * blocks, LANES:] for k in range(5)]
    tr, ti = [re[0]], [None]
    for k in range(1, 5):
        c, s = tw[k - 1 : k, :], tw[k + 3 : k + 4, :]
        tr.append(re[k] * c + im[k] * s)
        ti.append(re[k] * s - im[k] * c)
    plus, minus = tr[0] + tr[4], tr[0] - tr[4]
    p1, m1 = (tr[1] + ti[1]) * ROOT_HALF, (tr[1] - ti[1]) * ROOT_HALF
    p3, m3 = (tr[3] + ti[3]) * ROOT_HALF, (tr[3] - ti[3]) * ROOT_HALF
    e0, e1 = plus + tr[2], tr[1] + tr[3]
    f0, f1 = plus - tr[2], ti[3] - ti[1]
    g0, g1 = minus - ti[2], m1 - p3
    h0, h1 = minus + ti[2], m3 - p1
    return [e0 + e1, g0 + g1, f0 + f1, h0 + h1, e0 - e1, g0 - g1, f0 - f1, h0 - h1]


def local_kernel(
    patches, x_ref, angle_ref, offset_ref, patch_ref, block_ref, spec_ref, table_ref, tw_ref,
    out_ref, val_ref, low_ref, high_ref, binned_ref,
):
    blocks, length = x_ref.shape
    x = x_ref[...]
    filtered = filter_blocks(x, spec_ref, table_ref[...], tw_ref[...])
    total = jnp.zeros((blocks, LANES), F32)
    for i in range(RADIX):
        at = slice(i * LANES, (i + 1) * LANES)
        f = filtered[i]
        total = total + x[:, at] * f
        odd, c, s = double_angle(angle_ref[:, at])
        turned = jnp.where(odd, -f, f)
        for comp, v in enumerate((f, turned * c, turned * s)):
            hi, lo = split2(v)
            val_ref[comp, :, at] = hi
            val_ref[3 + comp, :, at] = lo
        off = offset_ref[:, at]
        low_ref[:, at] = (off & (LOW - 1)).astype(F32).astype(BF16)
        high_ref[:, at] = (off >> 4).astype(F32).astype(BF16)
    curvature = jnp.sum(jnp.sum(total, axis=0, keepdims=True), axis=1, keepdims=True)

    lane = iota((GROUP, LANES), 1) % 16

    def one_group(g, carry):
        rows = pl.ds(pl.multiple_of(g * GROUP, GROUP), GROUP)
        low, high = low_ref[rows, :], high_ref[rows, :]
        ones = jnp.concatenate(
            [jnp.where(low == k, 1.0, 0.0).astype(BF16) for k in range(LOW)], axis=0
        )
        masks = [high == k for k in range(HIGH)]
        values = []
        for comp in range(6):
            v = val_ref[comp, rows, :]
            values += [jnp.where(masks[k], v, jnp.zeros_like(v)) for k in range(HIGH)]
        got = dot_nt(jnp.concatenate(values, axis=0), ones)
        half = 3 * HIGH * GROUP
        got = got[:half, :] + got[half:, :]
        for h in range(2):
            acc = jnp.zeros((GROUP, LANES), F32)
            for sa in range(3 * HIGH):
                piece = got[sa * GROUP : (sa + 1) * GROUP, h * LANES : (h + 1) * LANES]
                moved = jnp.concatenate(
                    [
                        pltpu.roll(piece[:8], sa, 1, stride=15, stride_axis=0),
                        pltpu.roll(piece[8:], sa + 8, 1, stride=15, stride_axis=0),
                    ],
                    axis=0,
                )
                acc = jnp.where(lane == sa, moved, acc)
            binned_ref[rows, h * LANES : (h + 1) * LANES] = acc
        return carry

    lax.fori_loop(0, blocks // GROUP, one_group, 0)

    capacity = 2 * blocks // patches
    patch_row = patch_ref[...].astype(F32)
    patch_col = jnp.broadcast_to(patch_row, (blocks, blocks)).T
    block_col = jnp.broadcast_to(block_ref[...].astype(F32), (blocks, blocks)).T
    earlier = iota((blocks, blocks), 0) < iota((blocks, blocks), 1)
    same = jnp.where((patch_col == patch_row) & earlier, 1.0, 0.0)
    position = patch_row * capacity + jnp.sum(same, axis=0, keepdims=True)
    select = (iota((2 * blocks, blocks), 0).astype(F32) == position).astype(F32).astype(BF16)
    turned = iota((blocks, LANES), 0)
    turned = turned + (turned >> 3 & 1)
    halves = []
    for h in range(2):
        part = binned_ref[:, h * LANES : (h + 1) * LANES]
        for bit in (1, 2, 4):
            part = jnp.where((turned & bit) != 0, pltpu.roll(part, LANES - 16 * bit, 1), part)
        halves.append(part)
    first = jnp.where(iota((blocks, LANES), 1) == LABEL_LANE, block_col + 1.0, halves[0])
    hi, lo = split2(jnp.concatenate([first, halves[1]], axis=1))
    payload = dot(jnp.concatenate([select, select], axis=1), jnp.concatenate([hi, lo], axis=0))
    out_ref[...] = jnp.where(iota(payload.shape, 1) == CURVE_LANE, curvature, payload)


def exchange(axis, count, me, send_at, recv_ref, send_sem, recv_sem):
    def one(step, carry):
        peer = lax.rem(me + step, count)
        pltpu.make_async_remote_copy(
            src_ref=send_at(peer),
            dst_ref=recv_ref.at[me],
            send_sem=send_sem,
            recv_sem=recv_sem,
            device_id={axis: peer},
            device_id_type=MESH,
        ).start()
        return carry

    lax.fori_loop(1, count, one, 0)
    pltpu.make_async_copy(send_at(me), recv_ref.at[me], recv_sem).start()
    pltpu.make_async_copy(recv_ref, recv_ref, recv_sem).wait()


def drain(count, recv_ref, send_sem):
    if count > 1:
        sent = recv_ref.at[pl.ds(0, count - 1)]
        pltpu.make_async_copy(sent, sent, send_sem).wait()


def link_kernel(
    patches, dets, pay_ref, res_ref, rz_ref, leg_ref, filt_ref, spread_ref, table_ref,
    new_ref, pre_ref, beta_ref,
    recv1, send2, recv2, send3, recv3, send4, recv4, send5, recv5, send_sems, recv_sems,
):
    my_patch, my_det = lax.axis_index("patch"), lax.axis_index("det")
    barrier = pltpu.get_barrier_semaphore()

    def greet(axis, count, me):
        def one(step, carry):
            pl.semaphore_signal(
                barrier, inc=1, device_id={axis: lax.rem(me + step, count)}, device_id_type=MESH
            )
            return carry

        lax.fori_loop(1, count, one, 0)

    greet("patch", patches, my_patch)
    greet("det", dets, my_det)
    pl.semaphore_wait(barrier, patches + dets - 2)

    capacity = recv1.shape[1]
    exchange(
        "patch", patches, my_patch, lambda p: pay_ref.at[p], recv1, send_sems.at[0], recv_sems.at[0]
    )
    got = recv1[...].reshape(patches * capacity, 256)
    hi, lo = split2(got)
    pick = (iota((16, LANES), 1) == LABEL_LANE).astype(F32).astype(BF16)
    labels = dot_nt(pick, hi[:, :LANES])[0:1, :]
    onehot = (iota((256, got.shape[0]), 0).astype(F32) + 1.0 == labels).astype(F32).astype(BF16)
    dense = dot(jnp.concatenate([onehot, onehot], axis=1), jnp.concatenate([hi, lo], axis=0))
    curve = jnp.sum(got, axis=0, keepdims=True) * (1.0 / capacity)
    dense = jnp.where(iota(dense.shape, 1) == CURVE_LANE, curve, dense)
    rows = 256 // dets
    send2[...] = dense.reshape(dets, rows, 256)
    exchange(
        "det", dets, my_det, lambda d: send2.at[d], recv2, send_sems.at[1], recv_sems.at[1]
    )
    image = jnp.sum(recv2[...], axis=0)
    rz_before = rz_ref[0]
    step_size = rz_before / image[0:1, CURVE_LANE : CURVE_LANE + 1]

    parts = split3(image)
    stacked = jnp.concatenate([p.astype(F32) for p in parts], axis=0).astype(BF16)
    wide = dot(stacked, spread_ref[...])
    wide = wide[:rows, :] + wide[rows : 2 * rows, :] + wide[2 * rows :, :]
    own_quarter = iota((rows, 256), 0) % 4 == iota((rows, 256), 1) // 64
    fields = []
    for s in range(3):
        old = res_ref[s]
        old = jnp.concatenate([old, old, old, old], axis=1)
        new = old - step_size * wide[:, s * 256 : (s + 1) * 256]
        new_ref[s] = new[:, :64]
        fields.append(jnp.where(own_quarter, new, 0.0))
    hi, lo = split2(jnp.concatenate(fields, axis=0))
    modes = dot(jnp.concatenate([hi, lo, hi], axis=1), table_ref[...])
    modes_here = LANES // dets
    slot = iota((dets, LANES), 1) // modes_here
    message = jnp.zeros((dets, LANES), F32)
    for ring in range(rows // 4):
        for s in range(3):
            at = s * rows + ring * 4
            line = jnp.sum(modes[at : at + 4, :], axis=0, keepdims=True)
            for e in range(2):
                target = ring * 16 + 2 * s + e
                wide_line = jnp.broadcast_to(line[:, e * LANES : (e + 1) * LANES], (dets, LANES))
                moved = pltpu.roll(wide_line, 0, 1, stride=modes_here, stride_axis=0)
                moved = pltpu.roll(moved, target * modes_here, 1)
                message = jnp.where(slot == target, moved, message)
    for d in range(dets):
        send3[d] = message[d : d + 1, :]
    exchange(
        "det", dets, my_det, lambda d: send3.at[d], recv3, send_sems.at[2], recv_sems.at[2]
    )

    cycles = recv3[...].reshape(dets, LANES)
    cycles = jnp.concatenate([cycles, pltpu.roll(cycles, 64, 1)], axis=0)
    cycles = jnp.concatenate([cycles, jnp.zeros((LANES - 2 * dets, LANES), F32)], axis=0).T
    columns = 6 * modes_here
    hi, lo = split2(cycles[: columns + 8, : 2 * dets])
    ring_of = iota((2 * dets, 2 * dets), 0)
    place = iota((2 * dets, 2 * dets), 1)
    order = (ring_of == 2 * (place % dets) + place // dets).astype(F32).astype(BF16)
    a, b, c = split3(leg_ref[...].reshape(modes_here * 64, 2 * dets))
    legendre = dot(a, order) + dot(b, order) + dot(c, order)
    leg_hi, leg_lo = split2(legendre)
    product = dot_nt(hi, leg_hi) + dot_nt(lo, leg_hi) + dot_nt(hi, leg_lo)
    mode_of = iota((columns, 64), 0) % modes_here
    coef = jnp.zeros((columns, 64), F32)
    for m in range(modes_here):
        coef = jnp.where(mode_of == m, product[:columns, m * 64 : (m + 1) * 64], coef)
    weight = jnp.concatenate([filt_ref[...]] * 6, axis=0)
    pre = weight * coef
    for c in range(6):
        pre_ref[c] = pre[c * modes_here : (c + 1) * modes_here, :]
    rz = jnp.sum(jnp.sum(pre * coef, axis=0, keepdims=True), axis=1, keepdims=True)
    send4[...] = jnp.broadcast_to(rz, (1, LANES))
    exchange("det", dets, my_det, lambda d: send4, recv4, send_sems.at[3], recv_sems.at[3])
    send5[...] = jnp.sum(recv4[...], axis=0)
    exchange("patch", patches, my_patch, lambda p: send5, recv5, send_sems.at[4], recv_sems.at[4])
    beta_ref[...] = jnp.sum(recv5[...], axis=0) / rz_before

    drain(patches, recv1, send_sems.at[0])
    drain(dets, recv2, send_sems.at[1])
    drain(dets, recv3, send_sems.at[2])
    drain(dets, recv4, send_sems.at[3])
    drain(patches, recv5, send_sems.at[4])


def per_device(
    patches, dets, tod_image, angles, pixel_offset, target_patch, target_block, noise_spectrum,
    residual, previous_rz, legendre, harmonic_filter,
):
    blocks, length = tod_image.shape[2:]
    vmem = pl.BlockSpec(memory_space=pltpu.VMEM)
    smem = pl.BlockSpec(memory_space=pltpu.SMEM)
    payload = pl.pallas_call(
        functools.partial(local_kernel, patches),
        out_shape=jax.ShapeDtypeStruct((2 * blocks, 256), F32),
        in_specs=[vmem] * 8,
        out_specs=vmem,
        scratch_shapes=[
            pltpu.VMEM((6, blocks, length), BF16),
            pltpu.VMEM((blocks, length), BF16),
            pltpu.VMEM((blocks, length), BF16),
            pltpu.VMEM((blocks, 256), F32),
        ],
        compiler_params=pltpu.CompilerParams(vmem_limit_bytes=40 * 1024 * 1024),
    )(
        tod_image[0, 0],
        angles[0, 0],
        pixel_offset[0, 0],
        target_patch.reshape(1, blocks),
        target_block.reshape(1, blocks),
        noise_spectrum[0, 0],
        jnp.asarray(fourier_matrix()),
        jnp.asarray(twiddle_rows()),
    )
    capacity = 2 * blocks // patches
    rows = residual.shape[1]
    modes_here = legendre.shape[0]
    new, pre, beta = pl.pallas_call(
        functools.partial(link_kernel, patches, dets),
        out_shape=(
            jax.ShapeDtypeStruct((3, rows, 64), F32),
            jax.ShapeDtypeStruct((6, modes_here, 64), F32),
            jax.ShapeDtypeStruct((1, LANES), F32),
        ),
        in_specs=[vmem, vmem, smem, vmem, vmem, vmem, vmem],
        out_specs=(vmem, vmem, vmem),
        scratch_shapes=[
            pltpu.VMEM((patches, capacity, 256), F32),
            pltpu.VMEM((dets, rows, 256), F32),
            pltpu.VMEM((dets, rows, 256), F32),
            pltpu.VMEM((dets, 1, LANES), F32),
            pltpu.VMEM((dets, 1, LANES), F32),
            pltpu.VMEM((1, LANES), F32),
            pltpu.VMEM((dets, 1, LANES), F32),
            pltpu.VMEM((1, LANES), F32),
            pltpu.VMEM((patches, 1, LANES), F32),
            pltpu.SemaphoreType.DMA((5,)),
            pltpu.SemaphoreType.DMA((5,)),
        ],
        compiler_params=pltpu.CompilerParams(
            collective_id=0, has_side_effects=True, vmem_limit_bytes=40 * 1024 * 1024
        ),
    )(
        payload.reshape(patches, capacity, 256),
        residual[0].transpose(1, 0, 2),
        previous_rz,
        legendre,
        harmonic_filter,
        jnp.asarray(pixel_spread()),
        jnp.asarray(cycle_matrix(modes_here)),
    )
    return new.transpose(1, 0, 2)[None], pre.transpose(1, 0, 2)[None], beta[0, :1]


def solution(mesh):
    placed = (
        P("patch", "det", None, None),
        P("patch", "det", None, None),
        P("patch", "det", None, None),
        P("patch", "det", None, None),
        P("patch", "det", None),
        P("patch", "det", None, None),
        P("patch", "det", None, None),
        P(),
        P("det", None, None),
        P("det", None),
    )
    return jax.shard_map(
        functools.partial(per_device, mesh.shape["patch"], mesh.shape["det"]),
        mesh=mesh,
        in_specs=placed,
        out_specs=(P("patch", "det", None, None), P("patch", "det", None, None), P()),
        check_vma=False,
    )
```

```python
import functools
import math

import jax
import jax.numpy as jnp
import numpy as np
from jax import lax
from jax.experimental import pallas as pl
from jax.experimental.pallas import tpu as pltpu
from jax.sharding import PartitionSpec as P

BF16 = jnp.bfloat16
F32 = jnp.float32
I32 = jnp.int32
MESH = pl.DeviceIdType.MESH
LANES = 128
RADIX = 8
GROUP = 16
HIGH = 4
LOW = 16
ROOT_HALF = math.sqrt(0.5)


def split2(x):
    hi = x.astype(BF16)
    return hi, (x - hi.astype(F32)).astype(BF16)


def split3(x):
    hi = x.astype(BF16)
    rest = x - hi.astype(F32)
    mid = rest.astype(BF16)
    return hi, mid, (rest - mid.astype(F32)).astype(BF16)


def dot(a, b):
    return lax.dot_general(a, b, (((1,), (0,)), ((), ())), preferred_element_type=F32)


def dot_nt(a, b):
    return lax.dot_general(a, b, (((1,), (1,)), ((), ())), preferred_element_type=F32)


def iota(shape, dim):
    return lax.broadcasted_iota(I32, shape, dim)


def stack_table(table):
    hi, lo = split2(table)
    return jnp.concatenate([hi, hi, lo], axis=0)


def fourier_matrix():
    j = np.arange(LANES)
    angle = 2.0 * np.pi * (np.outer(j, j) % LANES) / LANES
    c, s = np.cos(angle), np.sin(angle)
    return np.block([[c, -s], [s, c]]).astype(np.float32)


def twiddle_rows():
    n = np.arange(LANES)
    angle = [2.0 * np.pi * n * k / (RADIX * LANES) for k in range(1, 5)]
    return np.stack([np.cos(a) for a in angle] + [np.sin(a) for a in angle]).astype(np.float32)


def cycle_matrix(modes_here):
    f = np.arange(256)[:, None]
    lane = np.arange(LANES)
    mode = (-(lane // modes_here) % (LANES // modes_here)) * modes_here + lane % modes_here
    angle = 2.0 * np.pi * (f * mode % 256) / 256.0
    scale = math.sqrt(2.0 / 256.0)
    return (np.concatenate([np.cos(angle), np.sin(angle)], axis=1) * scale).astype(np.float32)


def mode_rows(modes_here):
    row = np.arange(256)[:, None]
    owner, e, m = row // (2 * modes_here), row // modes_here % 2, row % modes_here
    mode = owner * modes_here + m
    angle = 2.0 * np.pi * (np.arange(256) * mode % 256) / 256.0
    rows = np.where(e == 0, np.cos(angle), np.sin(angle)) * math.sqrt(2.0 / 256.0)
    return rows.astype(np.float32)


def pixel_order():
    col = iota((1, 256), 1)
    s, pixel = col // 64, col % 64
    a, c = pixel // LOW, pixel % LOW
    source = jnp.where(s < 3, (c // 8) * LANES + (c % 8) * 16 + s * HIGH + a, -1)
    return (iota((256, 256), 0) == source).astype(F32).astype(BF16)


def double_angle(theta):
    n = jnp.round(theta * (2.0 / math.pi))
    odd = (n.astype(I32) & 1) == 1
    hi = np.float32(math.pi / 2)
    lo = np.float32(math.pi / 2 - float(hi))
    r = (theta - n * hi) - n * lo
    y = r * r
    c = jnp.full_like(y, COS_POLY[-1])
    for coef in COS_POLY[-2::-1]:
        c = c * y + coef
    s = jnp.full_like(y, SIN_POLY[-1])
    for coef in SIN_POLY[-2::-1]:
        s = s * y + coef
    return odd, c, s * r


def fit_polys():
    top = (math.pi / 4) ** 2 * 1.0001
    y = top * 0.5 * (1.0 - np.cos(np.pi * (np.arange(400) + 0.5) / 400))
    r = np.sqrt(y)
    power = y[:, None] ** np.arange(6)
    cos_c = np.linalg.lstsq(power, np.cos(2 * r), rcond=None)[0]
    sin_c = np.linalg.lstsq(power[:, :5], np.sin(2 * r) / r, rcond=None)[0]
    return [float(np.float32(v)) for v in cos_c], [float(np.float32(v)) for v in sin_c]


COS_POLY, SIN_POLY = fit_polys()


def filter_blocks(x, spec_ref, table, tw):
    blocks = x.shape[0]
    dets = spec_ref.shape[0]
    t = [x[:, i * LANES : (i + 1) * LANES] for i in range(RADIX)]
    a = [t[i] + t[i + 4] for i in range(4)]
    b = [t[i] - t[i + 4] for i in range(4)]
    even, odd = a[0] + a[2], a[1] + a[3]
    diff, both = (b[1] - b[3]) * ROOT_HALF, (b[1] + b[3]) * ROOT_HALF
    y = [
        (even + odd, None),
        (b[0] + diff, -(b[2] + both)),
        (a[0] - a[2], a[3] - a[1]),
        (b[0] - diff, b[2] - both),
        (even - odd, None),
    ]
    rows = [jnp.concatenate([y[0][0], jnp.zeros_like(x[:, :LANES])], axis=1)]
    for k in range(1, 5):
        c, s = tw[k - 1 : k, :], tw[k + 3 : k + 4, :]
        re, im = y[k]
        if im is None:
            rows.append(jnp.concatenate([re * c, -(re * s)], axis=1))
        else:
            rows.append(jnp.concatenate([re * c + im * s, im * c - re * s], axis=1))
    hi, lo = split2(jnp.concatenate(rows, axis=0))
    spectrum = dot(jnp.concatenate([hi, lo, hi], axis=1), table)

    col = iota((1, 5 * LANES), 1)
    k_of, j_of = col // LANES, col % LANES
    order = k_of + RADIX * j_of
    place = jnp.minimum(order, RADIX * LANES - order)
    pick = (iota((512, 5 * LANES), 0) == place).astype(F32).astype(BF16)
    own = spec_ref[...]
    parts = split3(own[:, :512])
    weight = dot(parts[0], pick) + dot(parts[1], pick) + dot(parts[2], pick)
    weight = weight + jnp.where(place == 512, own[:, 512:513], 0.0)
    edge = (k_of == 0) | (k_of == 4)
    weight = weight * jnp.where(edge, 1.0 / 1024.0, 2.0 / 1024.0)

    per = blocks // dets
    scaled = []
    for k in range(5):
        w = weight[:, k * LANES : (k + 1) * LANES]
        w = jnp.concatenate([w, -w], axis=1)
        for d in range(dets):
            part = spectrum[k * blocks + d * per : k * blocks + (d + 1) * per, :]
            scaled.append(part * w[d : d + 1, :])
    hi, lo = split2(jnp.concatenate(scaled, axis=0))
    u = dot(jnp.concatenate([hi, lo, hi], axis=1), table)
    re = [u[k * blocks : (k + 1) * blocks, :LANES] for k in range(5)]
    im = [u[k * blocks : (k + 1) * blocks, LANES:] for k in range(5)]
    tr, ti = [re[0]], [None]
    for k in range(1, 5):
        c, s = tw[k - 1 : k, :], tw[k + 3 : k + 4, :]
        tr.append(re[k] * c + im[k] * s)
        ti.append(re[k] * s - im[k] * c)
    plus, minus = tr[0] + tr[4], tr[0] - tr[4]
    p1, m1 = (tr[1] + ti[1]) * ROOT_HALF, (tr[1] - ti[1]) * ROOT_HALF
    p3, m3 = (tr[3] + ti[3]) * ROOT_HALF, (tr[3] - ti[3]) * ROOT_HALF
    e0, e1 = plus + tr[2], tr[1] + tr[3]
    f0, f1 = plus - tr[2], ti[3] - ti[1]
    g0, g1 = minus - ti[2], m1 - p3
    h0, h1 = minus + ti[2], m3 - p1
    return [e0 + e1, g0 + g1, f0 + f1, h0 + h1, e0 - e1, g0 - g1, f0 - f1, h0 - h1]


def bin_blocks(filtered, angle_ref, offset_ref, val_ref, low_ref, high_ref, binned_ref):
    blocks = angle_ref.shape[0]
    for i in range(RADIX):
        at = slice(i * LANES, (i + 1) * LANES)
        f = filtered[i]
        odd, c, s = double_angle(angle_ref[:, at])
        turned = jnp.where(odd, -f, f)
        for comp, v in enumerate((f, turned * c, turned * s)):
            hi, lo = split2(v)
            val_ref[comp, :, at] = hi
            val_ref[3 + comp, :, at] = lo
        off = offset_ref[:, at]
        low_ref[:, at] = (off & (LOW - 1)).astype(F32).astype(BF16)
        high_ref[:, at] = (off >> 4).astype(F32).astype(BF16)
    lane = iota((GROUP, LANES), 1) % 16

    def one_group(g, carry):
        rows = pl.ds(pl.multiple_of(g * GROUP, GROUP), GROUP)
        low, high = low_ref[rows, :], high_ref[rows, :]
        ones = jnp.concatenate(
            [jnp.where(low == k, 1.0, 0.0).astype(BF16) for k in range(LOW)], axis=0
        )
        masks = [high == k for k in range(HIGH)]
        values = []
        for comp in range(6):
            v = val_ref[comp, rows, :]
            values += [jnp.where(masks[k], v, jnp.zeros_like(v)) for k in range(HIGH)]
        got = dot_nt(jnp.concatenate(values, axis=0), ones)
        half = 3 * HIGH * GROUP
        got = got[:half, :] + got[half:, :]
        for h in range(2):
            acc = jnp.zeros((GROUP, LANES), F32)
            for sa in range(3 * HIGH):
                piece = got[sa * GROUP : (sa + 1) * GROUP, h * LANES : (h + 1) * LANES]
                moved = jnp.concatenate(
                    [
                        pltpu.roll(piece[:8], sa, 1, stride=15, stride_axis=0),
                        pltpu.roll(piece[8:], sa + 8, 1, stride=15, stride_axis=0),
                    ],
                    axis=0,
                )
                acc = jnp.where(lane == sa, moved, acc)
            binned_ref[rows, h * LANES : (h + 1) * LANES] = acc
        return carry

    lax.fori_loop(0, blocks // GROUP, one_group, 0)
    turned = iota((blocks, LANES), 0)
    turned = turned + (turned >> 3 & 1)
    halves = []
    for h in range(2):
        part = binned_ref[:, h * LANES : (h + 1) * LANES]
        for bit in (1, 2, 4):
            part = jnp.where((turned & bit) != 0, pltpu.roll(part, LANES - 16 * bit, 1), part)
        halves.append(part)
    return jnp.concatenate(halves, axis=1)


def route(patches, binned, curvature, patch_row, block_row, order):
    blocks = binned.shape[0]
    capacity = 2 * blocks // patches
    quarter = capacity // 2
    hi, lo = split2(binned)
    moved = dot(jnp.concatenate([hi, lo], axis=1), jnp.concatenate([order, order], axis=0))
    patch_row = patch_row.astype(F32)
    block_row = block_row.astype(F32)
    patch_col = jnp.broadcast_to(patch_row, (blocks, blocks)).T
    same = patch_col == patch_row
    above = iota((blocks, blocks), 0)
    beside = iota((blocks, blocks), 1)
    slot_row = jnp.sum(jnp.where(same & (above < beside), 1.0, 0.0), axis=0, keepdims=True)
    slot_col = jnp.sum(jnp.where(same & (beside < above), 1.0, 0.0), axis=1, keepdims=True)
    place = patch_row * capacity + slot_row
    row = iota((2 * blocks, blocks), 0)
    own = row.astype(F32)
    first_half = row % capacity < quarter

    def choose(hit):
        return hit.astype(F32).astype(BF16)

    select = choose(own == place)
    select_a = choose((own == place) & first_half)
    select_b = choose((own + quarter == place) & first_half)
    hi, lo = split2(moved[:, :LANES])
    front = dot(jnp.concatenate([select, select], axis=1), jnp.concatenate([hi, lo], axis=0))
    back = moved[:, LANES:]
    hi, lo = split2(back)
    hi2, lo2 = split2(pltpu.roll(back, 64, 1))
    back = dot(
        jnp.concatenate([select_a, select_a, select_b, select_b], axis=1),
        jnp.concatenate([hi, lo, hi2, lo2], axis=0),
    )
    named = jnp.where((row // capacity).astype(F32) == patch_row, block_row + 1.0, 0.0)
    slot_lane = (iota((blocks, LANES), 1) % capacity).astype(F32)
    labels = dot(named.astype(BF16), choose(slot_col == slot_lane))
    labels = jnp.where(iota(labels.shape, 1) < 64, labels, curvature)
    back = jnp.where(iota(back.shape, 0) % capacity == quarter, labels, back)
    return front, back


def start_exchange(axis, count, me, send_at, recv_at, send_sem, recv_sem):
    def one(step, carry):
        peer = lax.rem(me + step, count)
        pltpu.make_async_remote_copy(
            src_ref=send_at(peer),
            dst_ref=recv_at(me),
            send_sem=send_sem,
            recv_sem=recv_sem,
            device_id={axis: peer},
            device_id_type=MESH,
        ).start()
        return carry

    lax.fori_loop(1, count, one, 0)
    pltpu.make_async_copy(send_at(me), recv_at(me), recv_sem).start()


def await_bytes(ref, sem):
    pltpu.make_async_copy(ref, ref, sem).wait()


def fold_rows(x, step):
    wrapped = pltpu.roll(pltpu.roll(x, x.shape[0] - step, 0), 64, 1)
    return jnp.where(iota(x.shape, 1) < 64, x, wrapped)


def legendre_columns(columns, legendre, modes_here):
    hi, lo = split2(columns)
    leg_hi, leg_lo = split2(legendre)
    product = dot_nt(hi, leg_hi) + dot_nt(lo, leg_hi) + dot_nt(hi, leg_lo)
    rows = 6 * modes_here
    mode_of = iota((rows, 64), 0) % modes_here
    coef = jnp.zeros((rows, 64), F32)
    for m in range(modes_here):
        coef = jnp.where(mode_of == m, product[:rows, m * 64 : (m + 1) * 64], coef)
    return coef


def step_kernel(patches, dets, *refs):
    hbm, refs = refs[:INPUTS], refs[INPUTS:]
    (new_ref, pre_ref, beta_ref), refs = refs[:3], refs[3:]
    held, refs = refs[:INPUTS], refs[INPUTS:]
    (
        val_ref, low_ref, high_ref, binned_ref,
        send1, recv1, send2, recv2, send3, recv3, send_map, recv_map, send4, recv4, send5, recv5,
        in_sems, send_sems, recv_sems,
    ) = refs
    my_patch, my_det = lax.axis_index("patch"), lax.axis_index("det")
    fetches = [
        pltpu.make_async_copy(src, dst, in_sems.at[i]) for i, (src, dst) in enumerate(zip(hbm, held))
    ]
    for fetch in fetches:
        fetch.start()
    barrier = pltpu.get_barrier_semaphore()

    def greet(axis, count, me):
        def one(step, carry):
            pl.semaphore_signal(
                barrier, inc=1, device_id={axis: lax.rem(me + step, count)}, device_id_type=MESH
            )
            return carry

        lax.fori_loop(1, count, one, 0)

    greet("patch", patches, my_patch)
    greet("det", dets, my_det)
    (
        x_ref, table_ref, tw_ref, spec_ref, angle_ref, offset_ref, patch_ref, block_ref,
        res_ref, cycle_ref, modes_ref, leg_ref, filt_ref, rz_ref,
    ) = held

    for fetch in fetches[:4]:
        fetch.wait()
    x = x_ref[...]
    filtered = filter_blocks(x, spec_ref, stack_table(table_ref[...]), tw_ref[...])
    total = jnp.zeros((x.shape[0], LANES), F32)
    for i in range(RADIX):
        total = total + x[:, i * LANES : (i + 1) * LANES] * filtered[i]
    curvature = jnp.sum(jnp.sum(total, axis=0, keepdims=True), axis=1, keepdims=True)
    for fetch in fetches[4:]:
        fetch.wait()
    binned = bin_blocks(filtered, angle_ref, offset_ref, val_ref, low_ref, high_ref, binned_ref)
    front, back = route(
        patches, binned, curvature, patch_ref[...], block_ref[...], pixel_order()
    )
    capacity = front.shape[0] // patches
    half = capacity // 2
    send1[:, :capacity, :] = front.reshape(patches, capacity, LANES)
    send1[:, capacity:, :] = back.reshape(patches, capacity, LANES)
    pl.semaphore_wait(barrier, patches + dets - 2)
    used1 = capacity + half + 1
    start_exchange(
        "patch", patches, my_patch,
        lambda p: send1.at[p, pl.ds(0, used1)], lambda p: recv1.at[p, pl.ds(0, used1)],
        send_sems.at[0], recv_sems.at[0],
    )

    rows = res_ref.shape[1]
    modes_here = LANES // dets
    lines = []
    for s in range(3):
        old = res_ref[s]
        for ring in range(rows // 4):
            lines.append(
                jnp.concatenate([old[ring * 4 + q : ring * 4 + q + 1, :] for q in range(4)], axis=1)
            )
    lines.append(jnp.zeros((8 - len(lines), 256), F32))
    hi, lo = split2(jnp.concatenate(lines, axis=0))
    modes = dot(jnp.concatenate([hi, lo, hi], axis=1), stack_table(cycle_ref[...]))
    slot = iota((dets, LANES), 1) // modes_here
    message = jnp.zeros((dets, LANES), F32)
    for s in range(3):
        for ring in range(rows // 4):
            at = s * (rows // 4) + ring
            for e in range(2):
                target = ring * 16 + 2 * s + e
                line = modes[at : at + 1, e * LANES : (e + 1) * LANES]
                moved = pltpu.roll(
                    jnp.broadcast_to(line, (dets, LANES)), 0, 1, stride=modes_here, stride_axis=0
                )
                moved = pltpu.roll(moved, target * modes_here, 1)
                message = jnp.where(slot == target, moved, message)
    for d in range(dets):
        send3[d] = message[d : d + 1, :]
    start_exchange(
        "det", dets, my_det, lambda d: send3.at[d], lambda d: recv3.at[d],
        send_sems.at[2], recv_sems.at[2],
    )

    await_bytes(recv1.at[:, pl.ds(0, used1)], recv_sems.at[0])
    got0 = recv1[:, :capacity, :].reshape(patches * capacity, LANES)
    got1 = recv1[:, capacity:, :]
    tags = jnp.sum(jnp.where(iota(got1.shape, 1) == half, got1, 0.0), axis=1)
    got1 = jnp.where(iota(got1.shape, 1) < half, got1, 0.0).reshape(patches * capacity, LANES)
    curve = jnp.sum(tags, axis=0, keepdims=True)
    tags = jnp.where(iota(tags.shape, 1) < 64, tags, pltpu.roll(tags, 64, 1))
    per = LANES // capacity
    labels = jnp.concatenate(
        [
            jnp.sum(
                jnp.where(iota(tags.shape, 1) // capacity + h * per == iota(tags.shape, 0), tags, 0.0),
                axis=0,
                keepdims=True,
            )
            for h in range(patches // per)
        ],
        axis=1,
    )
    labels_b = pltpu.roll(labels, labels.shape[1] - half, 1)
    hi, lo = split2(got0)
    rhs0 = jnp.concatenate([hi, lo], axis=0)
    hi, lo = split2(got1)
    hi2, lo2 = split2(pltpu.roll(got1, 64, 1))
    rhs1 = jnp.concatenate([hi, lo, hi2, lo2], axis=0)

    def spread(target):
        hit = (target == labels).astype(F32).astype(BF16)
        hit_b = (target == labels_b).astype(F32).astype(BF16)
        return (
            dot(jnp.concatenate([hit, hit], axis=1), rhs0),
            dot(jnp.concatenate([hit, hit, hit_b, hit_b], axis=1), rhs1),
        )

    row = iota((256, patches * capacity), 0)
    map0, map1 = spread((row % 64 * 4 + row // 64 + 1).astype(F32))
    left = iota((64, LANES), 1) < 64
    fields = []
    for s in range(3):
        source = map1 if s == 2 else map0
        tiles = []
        for h in range(2):
            a = source[h * 128 : h * 128 + 64, :]
            b = source[h * 128 + 64 : h * 128 + 128, :]
            if s == 1:
                tiles.append(jnp.where(left, pltpu.roll(a, 64, 1), b))
            else:
                tiles.append(jnp.where(left, a, pltpu.roll(b, 64, 1)))
        fields.append(jnp.concatenate(tiles, axis=1))
    hi, lo = split2(jnp.concatenate(fields, axis=0))
    mode_hi, mode_lo = split2(modes_ref[...])
    modes = dot_nt(
        jnp.concatenate([mode_hi, mode_lo, mode_hi], axis=1),
        jnp.concatenate([hi, hi, lo], axis=1),
    )
    group = 2 * modes_here
    modes1 = fold_rows(
        jnp.concatenate([modes[:, LANES:], jnp.zeros((256, 64), F32)], axis=1), modes_here
    )
    modes1 = jnp.where(iota(modes1.shape, 0) % group == modes_here, curve, modes1)
    send2[:, :group, :] = modes[:, :LANES].reshape(dets, group, LANES)
    send2[:, group:, :] = modes1.reshape(dets, group, LANES)
    used2 = group + modes_here + 1
    start_exchange(
        "det", dets, my_det,
        lambda d: send2.at[d, pl.ds(0, used2)], lambda d: recv2.at[d, pl.ds(0, used2)],
        send_sems.at[1], recv_sems.at[1],
    )

    map0, map1 = spread((row + 1).astype(F32))
    used_map = rows + rows // 2
    send_map[:, :rows, :] = map0.reshape(dets, rows, LANES)
    send_map[:, rows:, :] = fold_rows(map1, rows // 2).reshape(dets, rows, LANES)
    start_exchange(
        "det", dets, my_det,
        lambda d: send_map.at[d, pl.ds(0, used_map)], lambda d: recv_map.at[d, pl.ds(0, used_map)],
        send_sems.at[5], recv_sems.at[5],
    )

    await_bytes(recv3, recv_sems.at[2])
    cycles = recv3[...].reshape(dets, LANES)
    cycles = jnp.concatenate([cycles, pltpu.roll(cycles, 64, 1)], axis=0)
    cycles = jnp.concatenate([cycles, jnp.zeros((LANES - 2 * dets, LANES), F32)], axis=0).T
    columns = 6 * modes_here
    ring_of = iota((2 * dets, 2 * dets), 0)
    place = iota((2 * dets, 2 * dets), 1)
    order = (ring_of == 2 * (place % dets) + place // dets).astype(F32).astype(BF16)
    legendre = leg_ref[...].reshape(modes_here * 64, 2 * dets)
    a, b, c = split3(legendre)
    coef_old = legendre_columns(
        cycles[: columns + 8, : 2 * dets], dot(a, order) + dot(b, order) + dot(c, order), modes_here
    )
    weight = jnp.concatenate([filt_ref[...]] * 6, axis=0)
    rz_before = rz_ref[...]

    await_bytes(recv2.at[:, pl.ds(0, used2)], recv_sems.at[1])
    sum0 = jnp.sum(recv2[:, :group, :], axis=0)
    sum1 = jnp.sum(recv2[:, group:, :], axis=0)
    step_size = rz_before / sum1[modes_here : modes_here + 1, 64:65]
    turned0, turned1 = pltpu.roll(sum0, 64, 1), pltpu.roll(sum1, 64, 1)
    image_modes = jnp.concatenate(
        [sum0, turned0, sum1[:modes_here], turned1[:modes_here], jnp.zeros((8, LANES), F32)], axis=0
    )[:, :64]
    coef = coef_old - step_size * legendre_columns(image_modes, legendre, modes_here)
    pre = weight * coef
    rz = jnp.sum(jnp.sum(pre * coef, axis=0, keepdims=True), axis=1, keepdims=True)
    send4[...] = jnp.broadcast_to(rz, (1, LANES))
    start_exchange(
        "det", dets, my_det, lambda d: send4, lambda d: recv4.at[d], send_sems.at[3], recv_sems.at[3]
    )
    for c in range(6):
        pre_ref[c] = pre[c * modes_here : (c + 1) * modes_here, :]
    await_bytes(recv_map.at[:, pl.ds(0, used_map)], recv_sems.at[5])
    image0 = jnp.sum(recv_map[:, :rows, :], axis=0)
    image1 = jnp.sum(recv_map[:, rows:, :], axis=0)
    low = rows // 2
    image1 = jnp.concatenate([image1[:low], pltpu.roll(image1, 64, 1)[:low]], axis=0)
    new_ref[0] = res_ref[0] - step_size * image0[:, :64]
    new_ref[1] = res_ref[1] - step_size * pltpu.roll(image0, 64, 1)[:, :64]
    new_ref[2] = res_ref[2] - step_size * image1[:, :64]

    await_bytes(recv4, recv_sems.at[3])
    send5[...] = jnp.sum(recv4[...], axis=0)
    start_exchange(
        "patch", patches, my_patch, lambda p: send5, lambda p: recv5.at[p],
        send_sems.at[4], recv_sems.at[4],
    )
    await_bytes(recv5, recv_sems.at[4])
    beta_ref[...] = jnp.sum(recv5[...], axis=0) / rz_before

    others = pl.ds(0, patches - 1)
    await_bytes(recv1.at[others, pl.ds(0, used1)], send_sems.at[0])
    await_bytes(recv5.at[others], send_sems.at[4])
    others = pl.ds(0, dets - 1)
    await_bytes(recv2.at[others, pl.ds(0, used2)], send_sems.at[1])
    await_bytes(recv3.at[others], send_sems.at[2])
    await_bytes(recv4.at[others], send_sems.at[3])
    await_bytes(recv_map.at[others, pl.ds(0, used_map)], send_sems.at[5])


INPUTS = 14


def per_device(
    patches, dets, tod_image, angles, pixel_offset, target_patch, target_block, noise_spectrum,
    residual, previous_rz, legendre, harmonic_filter,
):
    blocks, length = tod_image.shape[2:]
    vmem = pl.BlockSpec(memory_space=pltpu.VMEM)
    hbm = pl.BlockSpec(memory_space=pl.ANY)
    capacity = 2 * blocks // patches
    rows = residual.shape[1]
    modes_here = legendre.shape[0]
    operands = (
        tod_image[0, 0],
        jnp.asarray(fourier_matrix()),
        jnp.asarray(twiddle_rows()),
        noise_spectrum[0, 0],
        angles[0, 0],
        pixel_offset[0, 0],
        target_patch.reshape(1, blocks),
        target_block.reshape(1, blocks),
        residual[0].transpose(1, 0, 2),
        jnp.asarray(cycle_matrix(modes_here)),
        jnp.asarray(mode_rows(modes_here)),
        legendre,
        harmonic_filter,
        previous_rz.reshape(1, 1),
    )
    new, pre, beta = pl.pallas_call(
        functools.partial(step_kernel, patches, dets),
        out_shape=(
            jax.ShapeDtypeStruct((3, rows, 64), F32),
            jax.ShapeDtypeStruct((6, modes_here, 64), F32),
            jax.ShapeDtypeStruct((1, LANES), F32),
        ),
        in_specs=[hbm] * INPUTS,
        out_specs=(vmem, vmem, vmem),
        scratch_shapes=[pltpu.VMEM(a.shape, a.dtype) for a in operands]
        + [
            pltpu.VMEM((6, blocks, length), BF16),
            pltpu.VMEM((blocks, length), BF16),
            pltpu.VMEM((blocks, length), BF16),
            pltpu.VMEM((blocks, 256), F32),
            pltpu.VMEM((patches, 2 * capacity, LANES), F32),
            pltpu.VMEM((patches, 2 * capacity, LANES), F32),
            pltpu.VMEM((dets, 4 * modes_here, LANES), F32),
            pltpu.VMEM((dets, 4 * modes_here, LANES), F32),
            pltpu.VMEM((dets, 1, LANES), F32),
            pltpu.VMEM((dets, 1, LANES), F32),
            pltpu.VMEM((dets, 2 * rows, LANES), F32),
            pltpu.VMEM((dets, 2 * rows, LANES), F32),
            pltpu.VMEM((1, LANES), F32),
            pltpu.VMEM((dets, 1, LANES), F32),
            pltpu.VMEM((1, LANES), F32),
            pltpu.VMEM((patches, 1, LANES), F32),
            pltpu.SemaphoreType.DMA((INPUTS,)),
            pltpu.SemaphoreType.DMA((6,)),
            pltpu.SemaphoreType.DMA((6,)),
        ],
        compiler_params=pltpu.CompilerParams(
            collective_id=0, has_side_effects=True, vmem_limit_bytes=56 * 1024 * 1024
        ),
    )(*operands)
    return new.transpose(1, 0, 2)[None], pre.transpose(1, 0, 2)[None], beta[0, :1]


def solution(mesh):
    placed = (
        P("patch", "det", None, None),
        P("patch", "det", None, None),
        P("patch", "det", None, None),
        P("patch", "det", None, None),
        P("patch", "det", None),
        P("patch", "det", None, None),
        P("patch", "det", None, None),
        P(),
        P("det", None, None),
        P("det", None),
    )
    return jax.shard_map(
        functools.partial(per_device, mesh.shape["patch"], mesh.shape["det"]),
        mesh=mesh,
        in_specs=placed,
        out_specs=(P("patch", "det", None, None), P("patch", "det", None, None), P()),
        check_vma=False,
    )
```

```python
import functools
import math

import jax
import jax.numpy as jnp
import numpy as np
from jax import lax
from jax.experimental import pallas as pl
from jax.experimental.pallas import tpu as pltpu
from jax.sharding import PartitionSpec as P

BF16 = jnp.bfloat16
F32 = jnp.float32
I32 = jnp.int32
MESH = pl.DeviceIdType.MESH
LANES = 128
RADIX = 8
GROUP = 16
HIGH = 4
LOW = 16
ROOT_HALF = math.sqrt(0.5)


def split2(x):
    hi = x.astype(BF16)
    return hi, (x - hi.astype(F32)).astype(BF16)


def split3(x):
    hi = x.astype(BF16)
    rest = x - hi.astype(F32)
    mid = rest.astype(BF16)
    return hi, mid, (rest - mid.astype(F32)).astype(BF16)


def dot(a, b):
    return lax.dot_general(a, b, (((1,), (0,)), ((), ())), preferred_element_type=F32)


def dot_nt(a, b):
    return lax.dot_general(a, b, (((1,), (1,)), ((), ())), preferred_element_type=F32)


def iota(shape, dim):
    return lax.broadcasted_iota(I32, shape, dim)


def stack_table(table):
    hi, lo = split2(table)
    return jnp.concatenate([hi, hi, lo], axis=0)


def fourier_matrix():
    j = np.arange(LANES)
    angle = 2.0 * np.pi * (np.outer(j, j) % LANES) / LANES
    c, s = np.cos(angle), np.sin(angle)
    return np.concatenate([c, s], axis=1).astype(np.float32)


def twiddle_rows():
    n = np.arange(LANES)
    angle = [2.0 * np.pi * n * k / (RADIX * LANES) for k in range(1, 5)]
    return np.stack([np.cos(a) for a in angle] + [np.sin(a) for a in angle]).astype(np.float32)


def cycle_matrix(modes_here):
    f = np.arange(256)[:, None]
    lane = np.arange(LANES)
    mode = (-(lane // modes_here) % (LANES // modes_here)) * modes_here + lane % modes_here
    angle = 2.0 * np.pi * (f * mode % 256) / 256.0
    scale = math.sqrt(2.0 / 256.0)
    return (np.concatenate([np.cos(angle), np.sin(angle)], axis=1) * scale).astype(np.float32)


def mode_rows(modes_here):
    row = np.arange(256)[:, None]
    owner, e, m = row // (2 * modes_here), row // modes_here % 2, row % modes_here
    mode = owner * modes_here + m
    angle = 2.0 * np.pi * (np.arange(256) * mode % 256) / 256.0
    rows = np.where(e == 0, np.cos(angle), np.sin(angle)) * math.sqrt(2.0 / 256.0)
    return rows.astype(np.float32)


def pixel_order():
    col = iota((1, 256), 1)
    s, pixel = col // 64, col % 64
    a, c = pixel // LOW, pixel % LOW
    source = jnp.where(s < 3, (c // 8) * LANES + (c % 8) * 16 + s * HIGH + a, -1)
    return (iota((256, 256), 0) == source).astype(F32).astype(BF16)


def double_angle(theta):
    n = jnp.round(theta * (2.0 / math.pi))
    odd = (n.astype(I32) & 1) == 1
    hi = np.float32(math.pi / 2)
    lo = np.float32(math.pi / 2 - float(hi))
    r = (theta - n * hi) - n * lo
    y = r * r
    c = jnp.full_like(y, COS_POLY[-1])
    for coef in COS_POLY[-2::-1]:
        c = c * y + coef
    s = jnp.full_like(y, SIN_POLY[-1])
    for coef in SIN_POLY[-2::-1]:
        s = s * y + coef
    return odd, c, s * r


def fit_polys():
    top = (math.pi / 4) ** 2 * 1.0001
    y = top * 0.5 * (1.0 - np.cos(np.pi * (np.arange(400) + 0.5) / 400))
    r = np.sqrt(y)
    power = y[:, None] ** np.arange(6)
    cos_c = np.linalg.lstsq(power, np.cos(2 * r), rcond=None)[0]
    sin_c = np.linalg.lstsq(power[:, :5], np.sin(2 * r) / r, rcond=None)[0]
    return [float(np.float32(v)) for v in cos_c], [float(np.float32(v)) for v in sin_c]


COS_POLY, SIN_POLY = fit_polys()


def noise_weights(own):
    col = iota((1, 5 * LANES), 1)
    k_of, j_of = col // LANES, col % LANES
    order = k_of + RADIX * j_of
    place = jnp.minimum(order, RADIX * LANES - order)
    pick = (iota((512, 5 * LANES), 0) == place).astype(F32).astype(BF16)
    parts = split3(own[:, :512])
    weight = dot(parts[0], pick) + dot(parts[1], pick) + dot(parts[2], pick)
    weight = weight + jnp.where(place == 512, own[:, 512:513], 0.0)
    edge = (k_of == 0) | (k_of == 4)
    return weight * jnp.where(edge, 1.0 / 1024.0, 2.0 / 1024.0)


def filter_blocks(x, weight, table, tw):
    blocks = x.shape[0]
    dets = weight.shape[0]
    t = [x[:, i * LANES : (i + 1) * LANES] for i in range(RADIX)]
    a = [t[i] + t[i + 4] for i in range(4)]
    b = [t[i] - t[i + 4] for i in range(4)]
    even, odd = a[0] + a[2], a[1] + a[3]
    diff, both = (b[1] - b[3]) * ROOT_HALF, (b[1] + b[3]) * ROOT_HALF
    y = [
        (even + odd, None),
        (b[0] + diff, -(b[2] + both)),
        (a[0] - a[2], a[3] - a[1]),
        (b[0] - diff, b[2] - both),
        (even - odd, None),
    ]
    rows = [jnp.concatenate([y[0][0], jnp.zeros_like(x[:, :LANES])], axis=1)]
    for k in range(1, 5):
        c, s = tw[k - 1 : k, :], tw[k + 3 : k + 4, :]
        re, im = y[k]
        if im is None:
            rows.append(jnp.concatenate([re * c, -(re * s)], axis=1))
        else:
            rows.append(jnp.concatenate([re * c + im * s, im * c - re * s], axis=1))
    hi, lo = split2(jnp.concatenate(rows, axis=0))
    spectrum = dot(jnp.concatenate([hi, lo, hi], axis=1), table)

    per = blocks // dets
    scaled = []
    for k in range(5):
        w = weight[:, k * LANES : (k + 1) * LANES]
        w = jnp.concatenate([w, -w], axis=1)
        for d in range(dets):
            part = spectrum[k * blocks + d * per : k * blocks + (d + 1) * per, :]
            scaled.append(part * w[d : d + 1, :])
    hi, lo = split2(jnp.concatenate(scaled, axis=0))
    u = dot(jnp.concatenate([hi, lo, hi], axis=1), table)
    re = [u[k * blocks : (k + 1) * blocks, :LANES] for k in range(5)]
    im = [u[k * blocks : (k + 1) * blocks, LANES:] for k in range(5)]
    tr, ti = [re[0]], [None]
    for k in range(1, 5):
        c, s = tw[k - 1 : k, :], tw[k + 3 : k + 4, :]
        tr.append(re[k] * c + im[k] * s)
        ti.append(re[k] * s - im[k] * c)
    plus, minus = tr[0] + tr[4], tr[0] - tr[4]
    p1, m1 = (tr[1] + ti[1]) * ROOT_HALF, (tr[1] - ti[1]) * ROOT_HALF
    p3, m3 = (tr[3] + ti[3]) * ROOT_HALF, (tr[3] - ti[3]) * ROOT_HALF
    e0, e1 = plus + tr[2], tr[1] + tr[3]
    f0, f1 = plus - tr[2], ti[3] - ti[1]
    g0, g1 = minus - ti[2], m1 - p3
    h0, h1 = minus + ti[2], m3 - p1
    return [e0 + e1, g0 + g1, f0 + f1, h0 + h1, e0 - e1, g0 - g1, f0 - f1, h0 - h1]


def bin_blocks(filtered, angle_ref, offset_ref, val_ref, low_ref, high_ref, binned_ref):
    blocks = angle_ref.shape[0]
    for i in range(RADIX):
        at = slice(i * LANES, (i + 1) * LANES)
        f = filtered[i]
        odd, c, s = double_angle(angle_ref[:, at])
        turned = jnp.where(odd, -f, f)
        for comp, v in enumerate((f, turned * c, turned * s)):
            hi, lo = split2(v)
            val_ref[comp, :, at] = hi
            val_ref[3 + comp, :, at] = lo
        off = offset_ref[:, at]
        low_ref[:, at] = (off & (LOW - 1)).astype(F32).astype(BF16)
        high_ref[:, at] = (off >> 4).astype(F32).astype(BF16)
    lane = iota((GROUP, LANES), 1) % 16

    def one_group(g, carry):
        rows = pl.ds(pl.multiple_of(g * GROUP, GROUP), GROUP)
        low, high = low_ref[rows, :], high_ref[rows, :]
        one, none = jnp.ones_like(low), jnp.zeros_like(low)
        ones = jnp.concatenate([jnp.where(low == k, one, none) for k in range(LOW)], axis=0)
        masks = [high == k for k in range(HIGH)]
        values = []
        for comp in range(6):
            v = val_ref[comp, rows, :]
            values += [jnp.where(masks[k], v, none) for k in range(HIGH)]
        got = dot_nt(jnp.concatenate(values, axis=0), ones)
        half = 3 * HIGH * GROUP
        got = got[:half, :] + got[half:, :]
        for h in range(2):
            acc = jnp.zeros((GROUP, LANES), F32)
            for sa in range(3 * HIGH):
                piece = got[sa * GROUP : (sa + 1) * GROUP, h * LANES : (h + 1) * LANES]
                moved = jnp.concatenate(
                    [
                        pltpu.roll(piece[:8], sa, 1, stride=15, stride_axis=0),
                        pltpu.roll(piece[8:], sa + 8, 1, stride=15, stride_axis=0),
                    ],
                    axis=0,
                )
                acc = jnp.where(lane == sa, moved, acc)
            binned_ref[rows, h * LANES : (h + 1) * LANES] = acc
        return carry

    lax.fori_loop(0, blocks // GROUP, one_group, 0, unroll=blocks // GROUP)
    turned = iota((blocks, LANES), 0)
    turned = turned + (turned >> 3 & 1)
    halves = []
    for h in range(2):
        part = binned_ref[:, h * LANES : (h + 1) * LANES]
        for bit in (1, 2, 4):
            part = jnp.where((turned & bit) != 0, pltpu.roll(part, LANES - 16 * bit, 1), part)
        halves.append(part)
    return jnp.concatenate(halves, axis=1)


def plan_route(patches, patch_row, block_row):
    blocks = patch_row.shape[1]
    capacity = 2 * blocks // patches
    quarter = capacity // 2
    patch_row = patch_row.astype(F32)
    block_row = block_row.astype(F32)
    patch_col = jnp.broadcast_to(patch_row, (blocks, blocks)).T
    same = patch_col == patch_row
    above = iota((blocks, blocks), 0)
    beside = iota((blocks, blocks), 1)
    slot_row = jnp.sum(jnp.where(same & (above < beside), 1.0, 0.0), axis=0, keepdims=True)
    slot_col = jnp.sum(jnp.where(same & (beside < above), 1.0, 0.0), axis=1, keepdims=True)
    place = patch_row * capacity + slot_row
    row = iota((2 * blocks, blocks), 0)
    own = row.astype(F32)
    first_half = row % capacity < quarter

    def choose(hit):
        return hit.astype(F32).astype(BF16)

    select = choose(own == place)
    select_a = choose((own == place) & first_half)
    select_b = choose((own + quarter == place) & first_half)
    named = jnp.where((row // capacity).astype(F32) == patch_row, block_row + 1.0, 0.0)
    slot_lane = (iota((blocks, LANES), 1) % capacity).astype(F32)
    labels = dot(named.astype(BF16), choose(slot_col == slot_lane))
    return (
        jnp.concatenate([select, select], axis=1),
        jnp.concatenate([select_a, select_a, select_b, select_b], axis=1),
        labels,
    )


def route(patches, binned, curvature, order, selects):
    front_select, back_select, labels = selects
    capacity = 2 * binned.shape[0] // patches
    hi, lo = split2(binned)
    moved = dot(jnp.concatenate([hi, lo], axis=1), jnp.concatenate([order, order], axis=0))
    hi, lo = split2(moved[:, :LANES])
    front = dot(front_select, jnp.concatenate([hi, lo], axis=0))
    back = moved[:, LANES:]
    hi, lo = split2(back)
    hi2, lo2 = split2(pltpu.roll(back, 64, 1))
    back = dot(back_select, jnp.concatenate([hi, lo, hi2, lo2], axis=0))
    labels = jnp.where(iota(labels.shape, 1) < 64, labels, curvature)
    back = jnp.where(iota(back.shape, 0) % capacity == capacity // 2, labels, back)
    return front, back


class Place:
    def __init__(self, patches, dets):
        self.tall, self.wide = patches // 4, dets // 4
        self.patch, self.det = lax.axis_index("patch"), lax.axis_index("det")
        self.y, corner = lax.div(self.patch, 4), lax.rem(self.patch, 4)
        far, core = lax.div(corner, 2), lax.rem(corner, 2)
        self.x, near = lax.div(self.det, 4), lax.rem(self.det, 4)
        across = self.x * 4 + lax.rem(near + 2, 4)
        self.patch_inner = [
            ((1 - far) * 2 + (1 - core), across),
            ((1 - far) * 2 + core, across),
            (far * 2 + (1 - core), self.det),
            (corner, self.det),
        ]
        self.det_inner = [lax.rem(near + step, 4) for step in (2, 1, 3, 0)]

    def each_patch(self, act):
        def lines(outer, count):
            turned = self.y + self.tall // 2 + (1 - 2 * lax.rem(outer, 2)) * lax.div(outer + 1, 2)
            base = lax.rem(turned, self.tall) * 4
            for corner, det in self.patch_inner[:count]:
                act(base + corner, det, base + corner)

        self.walk(self.tall, lines)

    def each_det(self, act):
        def lines(outer, count):
            turned = self.x + self.wide // 2 + (1 - 2 * lax.rem(outer, 2)) * lax.div(outer + 1, 2)
            base = lax.rem(turned, self.wide) * 4
            for near in self.det_inner[:count]:
                act(self.patch, base + near, base + near)

        self.walk(self.wide, lines)

    def walk(self, count, lines):
        def one(outer, carry):
            lines(outer, 4)
            return carry

        lax.fori_loop(0, count - 1, one, 0)
        lines(jnp.int32(count - 1), 3)


def start_exchange(each, me, send_at, recv_at, send_sem, recv_sem):
    def act(patch, det, index):
        pltpu.make_async_remote_copy(
            src_ref=send_at(index),
            dst_ref=recv_at(me),
            send_sem=send_sem,
            recv_sem=recv_sem,
            device_id=(patch, det),
            device_id_type=MESH,
        ).start()

    each(act)
    pltpu.make_async_copy(send_at(me), recv_at(me), recv_sem).start()


def await_bytes(ref, sem):
    pltpu.make_async_copy(ref, ref, sem).wait()


def fold_rows(x, step):
    wrapped = pltpu.roll(pltpu.roll(x, x.shape[0] - step, 0), 64, 1)
    return jnp.where(iota(x.shape, 1) < 64, x, wrapped)


def legendre_columns(columns, legendre, modes_here):
    hi, lo = split2(columns)
    leg_hi, leg_lo = split2(legendre)
    product = dot_nt(hi, leg_hi) + dot_nt(lo, leg_hi) + dot_nt(hi, leg_lo)
    rows = 6 * modes_here
    mode_of = iota((rows, 64), 0) % modes_here
    coef = jnp.zeros((rows, 64), F32)
    for m in range(modes_here):
        coef = jnp.where(mode_of == m, product[:rows, m * 64 : (m + 1) * 64], coef)
    return coef


def step_kernel(patches, dets, *refs):
    hbm, refs = refs[:INPUTS], refs[INPUTS:]
    (new_ref, pre_ref, beta_ref), refs = refs[:3], refs[3:]
    held, refs = refs[:INPUTS], refs[INPUTS:]
    (
        val_ref, low_ref, high_ref, binned_ref,
        send1, recv1, send2, recv2, send3, recv3, send_map, recv_map, send4, recv4, send5, recv5,
        in_sems, send_sems, recv_sems,
    ) = refs
    place = Place(patches, dets)
    over_patch = (place.each_patch, place.patch)
    over_det = (place.each_det, place.det)
    fetches = [
        pltpu.make_async_copy(src, dst, in_sems.at[i]) for i, (src, dst) in enumerate(zip(hbm, held))
    ]
    for fetch in fetches[:FIRST]:
        fetch.start()
    barrier = pltpu.get_barrier_semaphore()

    def greet(patch, det, index):
        pl.semaphore_signal(barrier, inc=1, device_id=(patch, det), device_id_type=MESH)

    place.each_patch(greet)
    place.each_det(greet)
    (
        x_ref, table_ref, tw_ref, spec_ref, patch_ref, block_ref, angle_ref, offset_ref,
        res_ref, cycle_ref, modes_ref, leg_ref, filt_ref, rz_ref,
    ) = held

    for fetch in fetches[3:6]:
        fetch.wait()
    selects = plan_route(patches, patch_ref[...], block_ref[...])
    order = pixel_order()
    weight = noise_weights(spec_ref[...])
    for fetch in fetches[:3]:
        fetch.wait()
    for fetch in fetches[FIRST:]:
        fetch.start()
    x = x_ref[...]
    waves = table_ref[...]
    swapped = jnp.concatenate([waves[:, LANES:], waves[:, :LANES]], axis=1)
    signed = jnp.where(iota(waves.shape, 1) < LANES, waves, -waves)
    table = stack_table(jnp.concatenate([signed, swapped], axis=0))
    filtered = filter_blocks(x, weight, table, tw_ref[...])
    total = jnp.zeros((x.shape[0], LANES), F32)
    for i in range(RADIX):
        total = total + x[:, i * LANES : (i + 1) * LANES] * filtered[i]
    curvature = jnp.sum(jnp.sum(total, axis=0, keepdims=True), axis=1, keepdims=True)
    for fetch in fetches[FIRST : FIRST + 2]:
        fetch.wait()
    binned = bin_blocks(filtered, angle_ref, offset_ref, val_ref, low_ref, high_ref, binned_ref)
    front, back = route(patches, binned, curvature, order, selects)
    def drain(count, ref, index):
        await_bytes(ref.at[pl.ds(0, count - 1)], send_sems.at[index])

    capacity = front.shape[0] // patches
    half = capacity // 2
    send1[:, :capacity, :] = front.reshape(patches, capacity, LANES)
    send1[:, capacity:, :] = back.reshape(patches, capacity, LANES)
    pl.semaphore_wait(barrier, patches + dets - 2)
    used1 = capacity + half + 1
    start_exchange(
        *over_patch,
        lambda p: send1.at[p, pl.ds(0, used1)], lambda p: recv1.at[p, pl.ds(0, used1)],
        send_sems.at[0], recv_sems.at[0],
    )

    for fetch in fetches[FIRST + 2 :]:
        fetch.wait()
    rows = res_ref.shape[1]
    modes_here = LANES // dets
    lines = []
    for s in range(3):
        old = res_ref[s]
        for ring in range(rows // 4):
            lines.append(
                jnp.concatenate([old[ring * 4 + q : ring * 4 + q + 1, :] for q in range(4)], axis=1)
            )
    lines.append(jnp.zeros((8 - len(lines), 256), F32))
    hi, lo = split2(jnp.concatenate(lines, axis=0))
    modes = dot(jnp.concatenate([hi, lo, hi], axis=1), stack_table(cycle_ref[...]))
    slot = iota((dets, LANES), 1) // modes_here
    message = jnp.zeros((dets, LANES), F32)
    for s in range(3):
        for ring in range(rows // 4):
            at = s * (rows // 4) + ring
            for e in range(2):
                target = ring * 16 + 2 * s + e
                line = modes[at : at + 1, e * LANES : (e + 1) * LANES]
                moved = pltpu.roll(
                    jnp.broadcast_to(line, (dets, LANES)), 0, 1, stride=modes_here, stride_axis=0
                )
                moved = pltpu.roll(moved, target * modes_here, 1)
                message = jnp.where(slot == target, moved, message)
    for d in range(dets):
        send3[d] = message[d : d + 1, :]
    start_exchange(
        *over_det, lambda d: send3.at[d], lambda d: recv3.at[d],
        send_sems.at[2], recv_sems.at[2],
    )

    await_bytes(recv1.at[:, pl.ds(0, used1)], recv_sems.at[0])
    got0 = recv1[:, :capacity, :].reshape(patches * capacity, LANES)
    got1 = recv1[:, capacity:, :]
    tags = jnp.sum(jnp.where(iota(got1.shape, 1) == half, got1, 0.0), axis=1)
    got1 = jnp.where(iota(got1.shape, 1) < half, got1, 0.0).reshape(patches * capacity, LANES)
    curve = jnp.sum(tags, axis=0, keepdims=True)
    tags = jnp.where(iota(tags.shape, 1) < 64, tags, pltpu.roll(tags, 64, 1))
    per = LANES // capacity
    labels = jnp.concatenate(
        [
            jnp.sum(
                jnp.where(iota(tags.shape, 1) // capacity + h * per == iota(tags.shape, 0), tags, 0.0),
                axis=0,
                keepdims=True,
            )
            for h in range(patches // per)
        ],
        axis=1,
    )
    labels_b = pltpu.roll(labels, labels.shape[1] - half, 1)
    hi, lo = split2(got0)
    rhs0 = jnp.concatenate([hi, lo], axis=0)
    hi, lo = split2(got1)
    hi2, lo2 = split2(pltpu.roll(got1, 64, 1))
    rhs1 = jnp.concatenate([hi, lo, hi2, lo2], axis=0)

    def spread(target):
        hit = (target == labels).astype(F32).astype(BF16)
        hit_b = (target == labels_b).astype(F32).astype(BF16)
        return (
            dot(jnp.concatenate([hit, hit], axis=1), rhs0),
            dot(jnp.concatenate([hit, hit, hit_b, hit_b], axis=1), rhs1),
        )

    row = iota((256, patches * capacity), 0)
    map0, map1 = spread((row % 64 * 4 + row // 64 + 1).astype(F32))
    left = iota((64, LANES), 1) < 64
    fields = []
    for s in range(3):
        source = map1 if s == 2 else map0
        tiles = []
        for h in range(2):
            a = source[h * 128 : h * 128 + 64, :]
            b = source[h * 128 + 64 : h * 128 + 128, :]
            if s == 1:
                tiles.append(jnp.where(left, pltpu.roll(a, 64, 1), b))
            else:
                tiles.append(jnp.where(left, a, pltpu.roll(b, 64, 1)))
        fields.append(jnp.concatenate(tiles, axis=1))
    hi, lo = split2(jnp.concatenate(fields, axis=0))
    mode_hi, mode_lo = split2(modes_ref[...])
    modes = dot_nt(
        jnp.concatenate([mode_hi, mode_lo, mode_hi], axis=1),
        jnp.concatenate([hi, hi, lo], axis=1),
    )
    group = 2 * modes_here
    modes1 = fold_rows(
        jnp.concatenate([modes[:, LANES:], jnp.zeros((256, 64), F32)], axis=1), modes_here
    )
    modes1 = jnp.where(iota(modes1.shape, 0) % group == modes_here, curve, modes1)
    send2[:, :group, :] = modes[:, :LANES].reshape(dets, group, LANES)
    send2[:, group:, :] = modes1.reshape(dets, group, LANES)
    used2 = group + modes_here + 1
    start_exchange(
        *over_det,
        lambda d: send2.at[d, pl.ds(0, used2)], lambda d: recv2.at[d, pl.ds(0, used2)],
        send_sems.at[1], recv_sems.at[1],
    )

    map0, map1 = spread((row + 1).astype(F32))
    used_map = rows + rows // 2
    send_map[:, :rows, :] = map0.reshape(dets, rows, LANES)
    send_map[:, rows:, :] = fold_rows(map1, rows // 2).reshape(dets, rows, LANES)
    await_bytes(recv3, recv_sems.at[2])
    cycles = recv3[...].reshape(dets, LANES)
    cycles = jnp.concatenate([cycles, pltpu.roll(cycles, 64, 1)], axis=0)
    cycles = jnp.concatenate([cycles, jnp.zeros((LANES - 2 * dets, LANES), F32)], axis=0).T
    columns = 6 * modes_here
    ring_of = iota((2 * dets, 2 * dets), 0)
    column = iota((2 * dets, 2 * dets), 1)
    order = (ring_of == 2 * (column % dets) + column // dets).astype(F32).astype(BF16)
    legendre = leg_ref[...].reshape(modes_here * 64, 2 * dets)
    a, b, c = split3(legendre)
    coef_old = legendre_columns(
        cycles[: columns + 8, : 2 * dets], dot(a, order) + dot(b, order) + dot(c, order), modes_here
    )
    weight = jnp.concatenate([filt_ref[...]] * 6, axis=0)
    rz_before = rz_ref[...]

    await_bytes(recv2.at[:, pl.ds(0, used2)], recv_sems.at[1])
    sum0 = jnp.sum(recv2[:, :group, :], axis=0)
    sum1 = jnp.sum(recv2[:, group:, :], axis=0)
    step_size = rz_before / sum1[modes_here : modes_here + 1, 64:65]
    turned0, turned1 = pltpu.roll(sum0, 64, 1), pltpu.roll(sum1, 64, 1)
    image_modes = jnp.concatenate(
        [sum0, turned0, sum1[:modes_here], turned1[:modes_here], jnp.zeros((8, LANES), F32)], axis=0
    )[:, :64]
    coef = coef_old - step_size * legendre_columns(image_modes, legendre, modes_here)
    pre = weight * coef
    rz = jnp.sum(jnp.sum(pre * coef, axis=0, keepdims=True), axis=1, keepdims=True)
    send4[...] = jnp.broadcast_to(rz, (1, LANES))
    start_exchange(
        *over_det, lambda d: send4, lambda d: recv4.at[d], send_sems.at[3], recv_sems.at[3]
    )
    drain(dets, recv2.at[:, pl.ds(0, used2)], 1)
    start_exchange(
        *over_det,
        lambda d: send_map.at[d, pl.ds(0, used_map)], lambda d: recv_map.at[d, pl.ds(0, used_map)],
        send_sems.at[5], recv_sems.at[5],
    )
    for c in range(6):
        pre_ref[c] = pre[c * modes_here : (c + 1) * modes_here, :]

    await_bytes(recv4, recv_sems.at[3])
    send5[...] = jnp.sum(recv4[...], axis=0)
    start_exchange(
        *over_patch, lambda p: send5, lambda p: recv5.at[p],
        send_sems.at[4], recv_sems.at[4],
    )
    await_bytes(recv_map.at[:, pl.ds(0, used_map)], recv_sems.at[5])
    image0 = jnp.sum(recv_map[:, :rows, :], axis=0)
    image1 = jnp.sum(recv_map[:, rows:, :], axis=0)
    low = rows // 2
    image1 = jnp.concatenate([image1[:low], pltpu.roll(image1, 64, 1)[:low]], axis=0)
    new_ref[0] = res_ref[0] - step_size * image0[:, :64]
    new_ref[1] = res_ref[1] - step_size * pltpu.roll(image0, 64, 1)[:, :64]
    new_ref[2] = res_ref[2] - step_size * image1[:, :64]

    await_bytes(recv5, recv_sems.at[4])
    beta_ref[...] = jnp.sum(recv5[...], axis=0) / rz_before

    drain(patches, recv1.at[:, pl.ds(0, used1)], 0)
    drain(dets, recv3, 2)
    drain(dets, recv4, 3)
    drain(patches, recv5, 4)
    drain(dets, recv_map.at[:, pl.ds(0, used_map)], 5)


def finish_kernel(new_in, pre_in, beta_in, new_ref, pre_ref, beta_ref):
    new_ref[...] = new_in[...]
    pre_ref[...] = pre_in[...]
    beta_ref[...] = beta_in[:, :1]


INPUTS = 14
FIRST = 6


def per_device(
    patches, dets, tod_image, angles, pixel_offset, target_patch, target_block, noise_spectrum,
    residual, previous_rz, legendre, harmonic_filter,
):
    blocks, length = tod_image.shape[2:]
    vmem = pl.BlockSpec(memory_space=pltpu.VMEM)
    hbm = pl.BlockSpec(memory_space=pl.ANY)
    capacity = 2 * blocks // patches
    rows = residual.shape[1]
    modes_here = legendre.shape[0]
    operands = (
        tod_image[0, 0],
        jnp.asarray(fourier_matrix()),
        jnp.asarray(twiddle_rows()),
        noise_spectrum[0, 0],
        target_patch.reshape(1, blocks),
        target_block.reshape(1, blocks),
        angles[0, 0],
        pixel_offset[0, 0],
        residual[0].transpose(1, 0, 2),
        jnp.asarray(cycle_matrix(modes_here)),
        jnp.asarray(mode_rows(modes_here)),
        legendre,
        harmonic_filter,
        previous_rz.reshape(1, 1),
    )
    new, pre, beta = pl.pallas_call(
        functools.partial(step_kernel, patches, dets),
        out_shape=(
            pltpu.VMEM((3, rows, 64), F32),
            pltpu.VMEM((6, modes_here, 64), F32),
            pltpu.VMEM((1, LANES), F32),
        ),
        in_specs=[hbm] * INPUTS,
        out_specs=(vmem, vmem, vmem),
        scratch_shapes=[pltpu.VMEM(a.shape, a.dtype) for a in operands]
        + [
            pltpu.VMEM((6, blocks, length), BF16),
            pltpu.VMEM((blocks, length), BF16),
            pltpu.VMEM((blocks, length), BF16),
            pltpu.VMEM((blocks, 256), F32),
            pltpu.VMEM((patches, 2 * capacity, LANES), F32),
            pltpu.VMEM((patches, 2 * capacity, LANES), F32),
            pltpu.VMEM((dets, 4 * modes_here, LANES), F32),
            pltpu.VMEM((dets, 4 * modes_here, LANES), F32),
            pltpu.VMEM((dets, 1, LANES), F32),
            pltpu.VMEM((dets, 1, LANES), F32),
            pltpu.VMEM((dets, 2 * rows, LANES), F32),
            pltpu.VMEM((dets, 2 * rows, LANES), F32),
            pltpu.VMEM((1, LANES), F32),
            pltpu.VMEM((dets, 1, LANES), F32),
            pltpu.VMEM((1, LANES), F32),
            pltpu.VMEM((patches, 1, LANES), F32),
            pltpu.SemaphoreType.DMA((INPUTS,)),
            pltpu.SemaphoreType.DMA((6,)),
            pltpu.SemaphoreType.DMA((6,)),
        ],
        compiler_params=pltpu.CompilerParams(
            collective_id=0, has_side_effects=True, vmem_limit_bytes=56 * 1024 * 1024
        ),
    )(*operands)
    new, pre, beta = pl.pallas_call(
        finish_kernel,
        out_shape=(
            jax.ShapeDtypeStruct(new.shape, F32),
            jax.ShapeDtypeStruct(pre.shape, F32),
            jax.ShapeDtypeStruct((1, 1), F32),
        ),
        in_specs=[vmem] * 3,
        out_specs=(vmem,) * 3,
    )(new, pre, beta)
    return new.transpose(1, 0, 2)[None], pre.transpose(1, 0, 2)[None], beta.reshape(1)


def solution(mesh):
    placed = (
        P("patch", "det", None, None),
        P("patch", "det", None, None),
        P("patch", "det", None, None),
        P("patch", "det", None, None),
        P("patch", "det", None),
        P("patch", "det", None, None),
        P("patch", "det", None, None),
        P(),
        P("det", None, None),
        P("det", None),
    )
    return jax.shard_map(
        functools.partial(per_device, mesh.shape["patch"], mesh.shape["det"]),
        mesh=mesh,
        in_specs=placed,
        out_specs=(P("patch", "det", None, None), P("patch", "det", None, None), P()),
        check_vma=False,
    )
```

```python
import functools
import math

import jax
import jax.numpy as jnp
import numpy as np
from jax import lax
from jax.experimental import pallas as pl
from jax.experimental.pallas import tpu as pltpu
from jax.sharding import PartitionSpec as P

BF16 = jnp.bfloat16
F32 = jnp.float32
I32 = jnp.int32
MESH = pl.DeviceIdType.MESH
LANES = 128
RADIX = 8
GROUP = 16
HIGH = 4
LOW = 16
ROOT_HALF = math.sqrt(0.5)


def split2(x):
    hi = x.astype(BF16)
    return hi, (x - hi.astype(F32)).astype(BF16)


def split3(x):
    hi = x.astype(BF16)
    rest = x - hi.astype(F32)
    mid = rest.astype(BF16)
    return hi, mid, (rest - mid.astype(F32)).astype(BF16)


def dot(a, b):
    return lax.dot_general(a, b, (((1,), (0,)), ((), ())), preferred_element_type=F32)


def dot_nt(a, b):
    return lax.dot_general(a, b, (((1,), (1,)), ((), ())), preferred_element_type=F32)


def iota(shape, dim):
    return lax.broadcasted_iota(I32, shape, dim)


def stack_table(table):
    hi, lo = split2(table)
    return jnp.concatenate([hi, hi, lo], axis=0)


def fourier_matrix():
    j = np.arange(LANES)
    angle = 2.0 * np.pi * (np.outer(j, j) % LANES) / LANES
    c, s = np.cos(angle), np.sin(angle)
    return np.concatenate([c, s], axis=1).astype(np.float32)


def twiddle_rows():
    n = np.arange(LANES)
    angle = [2.0 * np.pi * n * k / (RADIX * LANES) for k in range(1, 5)]
    return np.stack([np.cos(a) for a in angle] + [np.sin(a) for a in angle]).astype(np.float32)


def cycle_matrix(modes_here):
    f = np.arange(256)[:, None]
    lane = np.arange(LANES)
    mode = (-(lane // modes_here) % (LANES // modes_here)) * modes_here + lane % modes_here
    angle = 2.0 * np.pi * (f * mode % 256) / 256.0
    scale = math.sqrt(2.0 / 256.0)
    return (np.concatenate([np.cos(angle), np.sin(angle)], axis=1) * scale).astype(np.float32)


def mode_rows(modes_here):
    row = np.arange(256)[:, None]
    owner, e, m = row // (2 * modes_here), row // modes_here % 2, row % modes_here
    mode = owner * modes_here + m
    angle = 2.0 * np.pi * (np.arange(256) * mode % 256) / 256.0
    rows = np.where(e == 0, np.cos(angle), np.sin(angle)) * math.sqrt(2.0 / 256.0)
    return rows.astype(np.float32)


def pixel_order():
    col = iota((1, 256), 1)
    s, pixel = col // 64, col % 64
    a, c = pixel // LOW, pixel % LOW
    source = jnp.where(s < 3, (c // 8) * LANES + (c % 8) * 16 + s * HIGH + a, -1)
    return (iota((256, 256), 0) == source).astype(F32).astype(BF16)


def double_angle(theta):
    n = jnp.round(theta * (2.0 / math.pi))
    odd = (n.astype(I32) & 1) == 1
    hi = np.float32(math.pi / 2)
    lo = np.float32(math.pi / 2 - float(hi))
    r = (theta - n * hi) - n * lo
    y = r * r
    c = jnp.full_like(y, COS_POLY[-1])
    for coef in COS_POLY[-2::-1]:
        c = c * y + coef
    s = jnp.full_like(y, SIN_POLY[-1])
    for coef in SIN_POLY[-2::-1]:
        s = s * y + coef
    return odd, c, s * r


def fit_polys():
    top = (math.pi / 4) ** 2 * 1.0001
    y = top * 0.5 * (1.0 - np.cos(np.pi * (np.arange(400) + 0.5) / 400))
    r = np.sqrt(y)
    power = y[:, None] ** np.arange(6)
    cos_c = np.linalg.lstsq(power, np.cos(2 * r), rcond=None)[0]
    sin_c = np.linalg.lstsq(power[:, :5], np.sin(2 * r) / r, rcond=None)[0]
    return [float(np.float32(v)) for v in cos_c], [float(np.float32(v)) for v in sin_c]


COS_POLY, SIN_POLY = fit_polys()


def noise_weights(own):
    col = iota((1, 5 * LANES), 1)
    k_of, j_of = col // LANES, col % LANES
    order = k_of + RADIX * j_of
    place = jnp.minimum(order, RADIX * LANES - order)
    pick = (iota((512, 5 * LANES), 0) == place).astype(F32).astype(BF16)
    dets = own.shape[0]
    parts = jnp.concatenate([part.astype(F32) for part in split3(own[:, :512])], axis=0)
    weight = dot(parts.astype(BF16), pick)
    weight = weight[:dets] + weight[dets : 2 * dets] + weight[2 * dets :]
    weight = weight + jnp.where(place == 512, own[:, 512:513], 0.0)
    edge = (k_of == 0) | (k_of == 4)
    return weight * jnp.where(edge, 1.0 / 1024.0, 2.0 / 1024.0)


def filter_blocks(x, weight, table, tw):
    blocks = x.shape[0]
    dets = weight.shape[0]
    t = [x[:, i * LANES : (i + 1) * LANES] for i in range(RADIX)]
    a = [t[i] + t[i + 4] for i in range(4)]
    b = [t[i] - t[i + 4] for i in range(4)]
    even, odd = a[0] + a[2], a[1] + a[3]
    diff, both = (b[1] - b[3]) * ROOT_HALF, (b[1] + b[3]) * ROOT_HALF
    y = [
        (even + odd, None),
        (b[0] + diff, -(b[2] + both)),
        (a[0] - a[2], a[3] - a[1]),
        (b[0] - diff, b[2] - both),
        (even - odd, None),
    ]
    rows = [jnp.concatenate([y[0][0], jnp.zeros_like(x[:, :LANES])], axis=1)]
    for k in range(1, 5):
        c, s = tw[k - 1 : k, :], tw[k + 3 : k + 4, :]
        re, im = y[k]
        if im is None:
            rows.append(jnp.concatenate([re * c, -(re * s)], axis=1))
        else:
            rows.append(jnp.concatenate([re * c + im * s, im * c - re * s], axis=1))
    hi, lo = split2(jnp.concatenate(rows, axis=0))
    spectrum = dot(jnp.concatenate([hi, lo, hi], axis=1), table)

    per = blocks // dets
    scaled = []
    for k in range(5):
        w = weight[:, k * LANES : (k + 1) * LANES]
        w = jnp.concatenate([w, -w], axis=1)
        for d in range(dets):
            part = spectrum[k * blocks + d * per : k * blocks + (d + 1) * per, :]
            scaled.append(part * w[d : d + 1, :])
    hi, lo = split2(jnp.concatenate(scaled, axis=0))
    u = dot(jnp.concatenate([hi, lo, hi], axis=1), table)
    re = [u[k * blocks : (k + 1) * blocks, :LANES] for k in range(5)]
    im = [u[k * blocks : (k + 1) * blocks, LANES:] for k in range(5)]
    tr, ti = [re[0]], [None]
    for k in range(1, 5):
        c, s = tw[k - 1 : k, :], tw[k + 3 : k + 4, :]
        tr.append(re[k] * c + im[k] * s)
        ti.append(re[k] * s - im[k] * c)
    plus, minus = tr[0] + tr[4], tr[0] - tr[4]
    p1, m1 = (tr[1] + ti[1]) * ROOT_HALF, (tr[1] - ti[1]) * ROOT_HALF
    p3, m3 = (tr[3] + ti[3]) * ROOT_HALF, (tr[3] - ti[3]) * ROOT_HALF
    e0, e1 = plus + tr[2], tr[1] + tr[3]
    f0, f1 = plus - tr[2], ti[3] - ti[1]
    g0, g1 = minus - ti[2], m1 - p3
    h0, h1 = minus + ti[2], m3 - p1
    return [e0 + e1, g0 + g1, f0 + f1, h0 + h1, e0 - e1, g0 - g1, f0 - f1, h0 - h1]


def bin_blocks(filtered, angle_ref, offset_ref, val_ref, low_ref, high_ref, binned_ref):
    blocks = angle_ref.shape[0]
    for i in range(RADIX):
        at = slice(i * LANES, (i + 1) * LANES)
        f = filtered[i]
        odd, c, s = double_angle(angle_ref[:, at])
        turned = jnp.where(odd, -f, f)
        for comp, v in enumerate((f, turned * c, turned * s)):
            hi, lo = split2(v)
            val_ref[comp, :, at] = hi
            val_ref[3 + comp, :, at] = lo
        off = offset_ref[:, at]
        low_ref[:, at] = (off & (LOW - 1)).astype(F32).astype(BF16)
        high_ref[:, at] = (off >> 4).astype(F32).astype(BF16)
    lane = iota((GROUP, LANES), 1) % 16

    def one_group(g, carry):
        rows = pl.ds(pl.multiple_of(g * GROUP, GROUP), GROUP)
        low, high = low_ref[rows, :], high_ref[rows, :]
        one, none = jnp.ones_like(low), jnp.zeros_like(low)
        ones = jnp.concatenate([jnp.where(low == k, one, none) for k in range(LOW)], axis=0)
        masks = [high == k for k in range(HIGH)]
        values = []
        for comp in range(6):
            v = val_ref[comp, rows, :]
            values += [jnp.where(masks[k], v, none) for k in range(HIGH)]
        got = dot_nt(jnp.concatenate(values, axis=0), ones)
        half = 3 * HIGH * GROUP
        got = got[:half, :] + got[half:, :]
        for h in range(2):
            acc = jnp.zeros((GROUP, LANES), F32)
            for sa in range(3 * HIGH):
                piece = got[sa * GROUP : (sa + 1) * GROUP, h * LANES : (h + 1) * LANES]
                moved = jnp.concatenate(
                    [
                        pltpu.roll(piece[:8], sa, 1, stride=15, stride_axis=0),
                        pltpu.roll(piece[8:], sa + 8, 1, stride=15, stride_axis=0),
                    ],
                    axis=0,
                )
                acc = jnp.where(lane == sa, moved, acc)
            binned_ref[rows, h * LANES : (h + 1) * LANES] = acc
        return carry

    lax.fori_loop(0, blocks // GROUP, one_group, 0, unroll=blocks // GROUP)
    turned = iota((blocks, LANES), 0)
    turned = turned + (turned >> 3 & 1)
    halves = []
    for h in range(2):
        part = binned_ref[:, h * LANES : (h + 1) * LANES]
        for bit in (1, 2, 4):
            part = jnp.where((turned & bit) != 0, pltpu.roll(part, LANES - 16 * bit, 1), part)
        halves.append(part)
    return jnp.concatenate(halves, axis=1)


def plan_route(patches, patch_row, block_row):
    blocks = patch_row.shape[1]
    capacity = 2 * blocks // patches
    quarter = capacity // 2
    patch_row = patch_row.astype(F32)
    block_row = block_row.astype(F32)
    patch_col = jnp.broadcast_to(patch_row, (blocks, blocks)).T
    same = patch_col == patch_row
    above = iota((blocks, blocks), 0)
    beside = iota((blocks, blocks), 1)
    slot_row = jnp.sum(jnp.where(same & (above < beside), 1.0, 0.0), axis=0, keepdims=True)
    slot_col = jnp.sum(jnp.where(same & (beside < above), 1.0, 0.0), axis=1, keepdims=True)
    place = patch_row * capacity + slot_row
    row = iota((2 * blocks, blocks), 0)
    own = row.astype(F32)
    first_half = row % capacity < quarter

    def choose(hit):
        return hit.astype(F32).astype(BF16)

    select = choose(own == place)
    select_a = choose((own == place) & first_half)
    select_b = choose((own + quarter == place) & first_half)
    named = jnp.where((row // capacity).astype(F32) == patch_row, block_row + 1.0, 0.0)
    slot_lane = (iota((blocks, LANES), 1) % capacity).astype(F32)
    labels = dot(named.astype(BF16), choose(slot_col == slot_lane))
    return (
        jnp.concatenate([select, select], axis=1),
        jnp.concatenate([select_a, select_a, select_b, select_b], axis=1),
        labels,
    )


def route(patches, binned, curvature, order, selects):
    front_select, back_select, labels = selects
    capacity = 2 * binned.shape[0] // patches
    hi, lo = split2(binned)
    moved = dot(jnp.concatenate([hi, lo], axis=1), jnp.concatenate([order, order], axis=0))
    hi, lo = split2(moved[:, :LANES])
    front = dot(front_select, jnp.concatenate([hi, lo], axis=0))
    back = moved[:, LANES:]
    hi, lo = split2(back)
    hi2, lo2 = split2(pltpu.roll(back, 64, 1))
    back = dot(back_select, jnp.concatenate([hi, lo, hi2, lo2], axis=0))
    labels = jnp.where(iota(labels.shape, 1) < 64, labels, curvature)
    back = jnp.where(iota(back.shape, 0) % capacity == capacity // 2, labels, back)
    return front, back


class Place:
    def __init__(self, patches, dets):
        self.tall, self.wide = patches // 4, dets // 4
        self.patch, self.det = lax.axis_index("patch"), lax.axis_index("det")
        self.y, corner = lax.div(self.patch, 4), lax.rem(self.patch, 4)
        far, core = lax.div(corner, 2), lax.rem(corner, 2)
        self.x, near = lax.div(self.det, 4), lax.rem(self.det, 4)
        across = self.x * 4 + lax.rem(near + 2, 4)
        self.patch_inner = [
            ((1 - far) * 2 + (1 - core), across),
            ((1 - far) * 2 + core, across),
            (far * 2 + (1 - core), self.det),
            (corner, self.det),
        ]
        self.det_inner = [lax.rem(near + step, 4) for step in (2, 1, 3, 0)]

    def each_patch(self, act):
        def lines(outer, count):
            turned = self.y + self.tall // 2 + (1 - 2 * lax.rem(outer, 2)) * lax.div(outer + 1, 2)
            base = lax.rem(turned, self.tall) * 4
            for corner, det in self.patch_inner[:count]:
                act(base + corner, det, base + corner)

        self.walk(self.tall, lines)

    def each_det(self, act):
        def lines(outer, count):
            turned = self.x + self.wide // 2 + (1 - 2 * lax.rem(outer, 2)) * lax.div(outer + 1, 2)
            base = lax.rem(turned, self.wide) * 4
            for near in self.det_inner[:count]:
                act(self.patch, base + near, base + near)

        self.walk(self.wide, lines)

    def walk(self, count, lines):
        def one(outer, carry):
            lines(outer, 4)
            return carry

        lax.fori_loop(0, count - 1, one, 0)
        lines(jnp.int32(count - 1), 3)


def start_exchange(each, me, send_at, recv_at, send_sem, recv_sem):
    def act(patch, det, index):
        pltpu.make_async_remote_copy(
            src_ref=send_at(index),
            dst_ref=recv_at(me),
            send_sem=send_sem,
            recv_sem=recv_sem,
            device_id=(patch, det),
            device_id_type=MESH,
        ).start()

    each(act)
    pltpu.make_async_copy(send_at(me), recv_at(me), recv_sem).start()


def await_bytes(ref, sem):
    pltpu.make_async_copy(ref, ref, sem).wait()


def fold_rows(x, step):
    wrapped = pltpu.roll(pltpu.roll(x, x.shape[0] - step, 0), 64, 1)
    return jnp.where(iota(x.shape, 1) < 64, x, wrapped)


def legendre_columns(columns, legendre, modes_here):
    hi, lo = split2(columns)
    leg_hi, leg_lo = split2(legendre)
    product = dot_nt(hi, leg_hi) + dot_nt(lo, leg_hi) + dot_nt(hi, leg_lo)
    rows = 6 * modes_here
    mode_of = iota((rows, 64), 0) % modes_here
    coef = jnp.zeros((rows, 64), F32)
    for m in range(modes_here):
        coef = jnp.where(mode_of == m, product[:rows, m * 64 : (m + 1) * 64], coef)
    return coef


def step_kernel(patches, dets, *refs):
    hbm, refs = refs[:INPUTS], refs[INPUTS:]
    (new_ref, pre_ref, beta_ref), refs = refs[:3], refs[3:]
    held, refs = refs[:INPUTS], refs[INPUTS:]
    (
        val_ref, low_ref, high_ref, binned_ref,
        send1, recv1, send2, recv2, send3, recv3, send_map, recv_map, send4, recv4, send5, recv5,
        in_sems, send_sems, recv_sems,
    ) = refs
    place = Place(patches, dets)
    over_patch = (place.each_patch, place.patch)
    over_det = (place.each_det, place.det)
    fetches = [
        pltpu.make_async_copy(src, dst, in_sems.at[i]) for i, (src, dst) in enumerate(zip(hbm, held))
    ]
    for fetch in fetches[:FIRST]:
        fetch.start()
    barrier = pltpu.get_barrier_semaphore()

    def greet(patch, det, index):
        pl.semaphore_signal(barrier, inc=1, device_id=(patch, det), device_id_type=MESH)

    place.each_patch(greet)
    place.each_det(greet)
    (
        x_ref, table_ref, tw_ref, spec_ref, patch_ref, block_ref, angle_ref, offset_ref,
        res_ref, cycle_ref, modes_ref, leg_ref, filt_ref, rz_ref,
    ) = held

    for fetch in fetches[3:6]:
        fetch.wait()
    selects = plan_route(patches, patch_ref[...], block_ref[...])
    order = pixel_order()
    weight = noise_weights(spec_ref[...])
    for fetch in fetches[:3]:
        fetch.wait()
    for fetch in fetches[FIRST : FIRST + 2]:
        fetch.start()
    x = x_ref[...]
    waves = table_ref[...]
    swapped = jnp.concatenate([waves[:, LANES:], waves[:, :LANES]], axis=1)
    signed = jnp.where(iota(waves.shape, 1) < LANES, waves, -waves)
    table = stack_table(jnp.concatenate([signed, swapped], axis=0))
    filtered = filter_blocks(x, weight, table, tw_ref[...])
    total = jnp.zeros((x.shape[0], LANES), F32)
    for i in range(RADIX):
        total = total + x[:, i * LANES : (i + 1) * LANES] * filtered[i]
    curvature = jnp.sum(jnp.sum(total, axis=0, keepdims=True), axis=1, keepdims=True)
    for fetch in fetches[FIRST : FIRST + 2]:
        fetch.wait()
    for fetch in fetches[FIRST + 2 :]:
        fetch.start()
    binned = bin_blocks(filtered, angle_ref, offset_ref, val_ref, low_ref, high_ref, binned_ref)
    front, back = route(patches, binned, curvature, order, selects)
    def drain(count, ref, index):
        await_bytes(ref.at[pl.ds(0, count - 1)], send_sems.at[index])

    capacity = front.shape[0] // patches
    half = capacity // 2
    send1[:, :capacity, :] = front.reshape(patches, capacity, LANES)
    send1[:, capacity:, :] = back.reshape(patches, capacity, LANES)
    pl.semaphore_wait(barrier, patches + dets - 2)
    used1 = capacity + half + 1
    start_exchange(
        *over_patch,
        lambda p: send1.at[p, pl.ds(0, used1)], lambda p: recv1.at[p, pl.ds(0, used1)],
        send_sems.at[0], recv_sems.at[0],
    )

    for fetch in fetches[FIRST + 2 :]:
        fetch.wait()
    rows = res_ref.shape[1]
    modes_here = LANES // dets
    lines = []
    for s in range(3):
        old = res_ref[s]
        for ring in range(rows // 4):
            lines.append(
                jnp.concatenate([old[ring * 4 + q : ring * 4 + q + 1, :] for q in range(4)], axis=1)
            )
    lines.append(jnp.zeros((8 - len(lines), 256), F32))
    hi, lo = split2(jnp.concatenate(lines, axis=0))
    modes = dot(jnp.concatenate([hi, lo, hi], axis=1), stack_table(cycle_ref[...]))
    slot = iota((dets, LANES), 1) // modes_here
    message = jnp.zeros((dets, LANES), F32)
    for s in range(3):
        for ring in range(rows // 4):
            at = s * (rows // 4) + ring
            for e in range(2):
                target = ring * 16 + 2 * s + e
                line = modes[at : at + 1, e * LANES : (e + 1) * LANES]
                moved = pltpu.roll(
                    jnp.broadcast_to(line, (dets, LANES)), 0, 1, stride=modes_here, stride_axis=0
                )
                moved = pltpu.roll(moved, target * modes_here, 1)
                message = jnp.where(slot == target, moved, message)
    for d in range(dets):
        send3[d] = message[d : d + 1, :]
    start_exchange(
        *over_det, lambda d: send3.at[d], lambda d: recv3.at[d],
        send_sems.at[2], recv_sems.at[2],
    )

    await_bytes(recv1.at[:, pl.ds(0, used1)], recv_sems.at[0])
    got0 = recv1[:, :capacity, :].reshape(patches * capacity, LANES)
    got1 = recv1[:, capacity:, :]
    tags = jnp.sum(jnp.where(iota(got1.shape, 1) == half, got1, 0.0), axis=1)
    got1 = jnp.where(iota(got1.shape, 1) < half, got1, 0.0).reshape(patches * capacity, LANES)
    curve = jnp.sum(tags, axis=0, keepdims=True)
    tags = jnp.where(iota(tags.shape, 1) < 64, tags, pltpu.roll(tags, 64, 1))
    per = LANES // capacity
    labels = jnp.concatenate(
        [
            jnp.sum(
                jnp.where(iota(tags.shape, 1) // capacity + h * per == iota(tags.shape, 0), tags, 0.0),
                axis=0,
                keepdims=True,
            )
            for h in range(patches // per)
        ],
        axis=1,
    )
    labels_b = pltpu.roll(labels, labels.shape[1] - half, 1)
    hi, lo = split2(got0)
    rhs0 = jnp.concatenate([hi, lo], axis=0)
    hi, lo = split2(got1)
    hi2, lo2 = split2(pltpu.roll(got1, 64, 1))
    rhs1 = jnp.concatenate([hi, lo, hi2, lo2], axis=0)

    def spread(target):
        hit = (target == labels).astype(F32).astype(BF16)
        hit_b = (target == labels_b).astype(F32).astype(BF16)
        return (
            dot(jnp.concatenate([hit, hit], axis=1), rhs0),
            dot(jnp.concatenate([hit, hit, hit_b, hit_b], axis=1), rhs1),
        )

    row = iota((256, patches * capacity), 0)
    map0, map1 = spread((row % 64 * 4 + row // 64 + 1).astype(F32))
    left = iota((64, LANES), 1) < 64
    fields = []
    for s in range(3):
        source = map1 if s == 2 else map0
        tiles = []
        for h in range(2):
            a = source[h * 128 : h * 128 + 64, :]
            b = source[h * 128 + 64 : h * 128 + 128, :]
            if s == 1:
                tiles.append(jnp.where(left, pltpu.roll(a, 64, 1), b))
            else:
                tiles.append(jnp.where(left, a, pltpu.roll(b, 64, 1)))
        fields.append(jnp.concatenate(tiles, axis=1))
    hi, lo = split2(jnp.concatenate(fields, axis=0))
    mode_hi, mode_lo = split2(modes_ref[...])
    modes = dot_nt(
        jnp.concatenate([mode_hi, mode_lo, mode_hi], axis=1),
        jnp.concatenate([hi, hi, lo], axis=1),
    )
    group = 2 * modes_here
    modes1 = fold_rows(
        jnp.concatenate([modes[:, LANES:], jnp.zeros((256, 64), F32)], axis=1), modes_here
    )
    modes1 = jnp.where(iota(modes1.shape, 0) % group == modes_here, curve, modes1)
    send2[:, :group, :] = modes[:, :LANES].reshape(dets, group, LANES)
    send2[:, group:, :] = modes1.reshape(dets, group, LANES)
    used2 = group + modes_here + 1
    start_exchange(
        *over_det,
        lambda d: send2.at[d, pl.ds(0, used2)], lambda d: recv2.at[d, pl.ds(0, used2)],
        send_sems.at[1], recv_sems.at[1],
    )

    map0, map1 = spread((row + 1).astype(F32))
    used_map = rows + rows // 2
    send_map[:, :rows, :] = map0.reshape(dets, rows, LANES)
    send_map[:, rows:, :] = fold_rows(map1, rows // 2).reshape(dets, rows, LANES)
    await_bytes(recv3, recv_sems.at[2])
    cycles = recv3[...].reshape(dets, LANES)
    cycles = jnp.concatenate([cycles, pltpu.roll(cycles, 64, 1)], axis=0)
    cycles = jnp.concatenate([cycles, jnp.zeros((LANES - 2 * dets, LANES), F32)], axis=0).T
    columns = 6 * modes_here
    ring_of = iota((2 * dets, 2 * dets), 0)
    column = iota((2 * dets, 2 * dets), 1)
    order = (ring_of == 2 * (column % dets) + column // dets).astype(F32).astype(BF16)
    legendre = leg_ref[...].reshape(modes_here * 64, 2 * dets)
    a, b, c = split3(legendre)
    coef_old = legendre_columns(
        cycles[: columns + 8, : 2 * dets], dot(a, order) + dot(b, order) + dot(c, order), modes_here
    )
    weight = jnp.concatenate([filt_ref[...]] * 6, axis=0)
    rz_before = rz_ref[0]

    await_bytes(recv2.at[:, pl.ds(0, used2)], recv_sems.at[1])
    sum0 = jnp.sum(recv2[:, :group, :], axis=0)
    sum1 = jnp.sum(recv2[:, group:, :], axis=0)
    step_size = rz_before / sum1[modes_here : modes_here + 1, 64:65]
    turned0, turned1 = pltpu.roll(sum0, 64, 1), pltpu.roll(sum1, 64, 1)
    image_modes = jnp.concatenate(
        [sum0, turned0, sum1[:modes_here], turned1[:modes_here], jnp.zeros((8, LANES), F32)], axis=0
    )[:, :64]
    coef = coef_old - step_size * legendre_columns(image_modes, legendre, modes_here)
    pre = weight * coef
    rz = jnp.sum(jnp.sum(pre * coef, axis=0, keepdims=True), axis=1, keepdims=True)
    send4[...] = jnp.broadcast_to(rz, (1, LANES))
    start_exchange(
        *over_det, lambda d: send4, lambda d: recv4.at[d], send_sems.at[3], recv_sems.at[3]
    )
    drain(dets, recv2.at[:, pl.ds(0, used2)], 1)
    start_exchange(
        *over_det,
        lambda d: send_map.at[d, pl.ds(0, used_map)], lambda d: recv_map.at[d, pl.ds(0, used_map)],
        send_sems.at[5], recv_sems.at[5],
    )
    for c in range(6):
        pre_ref[c] = pre[c * modes_here : (c + 1) * modes_here, :]

    await_bytes(recv4, recv_sems.at[3])
    send5[...] = jnp.sum(recv4[...], axis=0)
    start_exchange(
        *over_patch, lambda p: send5, lambda p: recv5.at[p],
        send_sems.at[4], recv_sems.at[4],
    )
    await_bytes(recv_map.at[:, pl.ds(0, used_map)], recv_sems.at[5])
    image0 = jnp.sum(recv_map[:, :rows, :], axis=0)
    image1 = jnp.sum(recv_map[:, rows:, :], axis=0)
    low = rows // 2
    image1 = jnp.concatenate([image1[:low], pltpu.roll(image1, 64, 1)[:low]], axis=0)
    new_ref[0] = res_ref[0] - step_size * image0[:, :64]
    new_ref[1] = res_ref[1] - step_size * pltpu.roll(image0, 64, 1)[:, :64]
    new_ref[2] = res_ref[2] - step_size * image1[:, :64]

    await_bytes(recv5, recv_sems.at[4])
    beta_ref[...] = jnp.sum(recv5[...], axis=0) / rz_before

    drain(patches, recv1.at[:, pl.ds(0, used1)], 0)
    drain(dets, recv3, 2)
    drain(dets, recv4, 3)
    drain(patches, recv5, 4)
    drain(dets, recv_map.at[:, pl.ds(0, used_map)], 5)


def finish_kernel(new_in, pre_in, beta_in, new_ref, pre_ref, beta_ref):
    new_ref[...] = new_in[...]
    pre_ref[...] = pre_in[...]
    beta_ref[...] = beta_in[:, :1]


INPUTS = 14
FIRST = 6


def per_device(
    patches, dets, tod_image, angles, pixel_offset, target_patch, target_block, noise_spectrum,
    residual, previous_rz, legendre, harmonic_filter,
):
    blocks, length = tod_image.shape[2:]
    vmem = pl.BlockSpec(memory_space=pltpu.VMEM)
    hbm = pl.BlockSpec(memory_space=pl.ANY)
    capacity = 2 * blocks // patches
    rows = residual.shape[1]
    modes_here = legendre.shape[0]
    operands = (
        tod_image[0, 0],
        jnp.asarray(fourier_matrix()),
        jnp.asarray(twiddle_rows()),
        noise_spectrum[0, 0],
        target_patch.reshape(1, blocks),
        target_block.reshape(1, blocks),
        angles[0, 0],
        pixel_offset[0, 0],
        residual[0].transpose(1, 0, 2),
        jnp.asarray(cycle_matrix(modes_here)),
        jnp.asarray(mode_rows(modes_here)),
        legendre,
        harmonic_filter,
        previous_rz,
    )
    new, pre, beta = pl.pallas_call(
        functools.partial(step_kernel, patches, dets),
        out_shape=(
            pltpu.VMEM((3, rows, 64), F32),
            pltpu.VMEM((6, modes_here, 64), F32),
            pltpu.VMEM((1, LANES), F32),
        ),
        in_specs=[hbm] * INPUTS,
        out_specs=(vmem, vmem, vmem),
        scratch_shapes=[pltpu.VMEM(a.shape, a.dtype) for a in operands[:-1]]
        + [pltpu.SMEM((1,), F32)]
        + [
            pltpu.VMEM((6, blocks, length), BF16),
            pltpu.VMEM((blocks, length), BF16),
            pltpu.VMEM((blocks, length), BF16),
            pltpu.VMEM((blocks, 256), F32),
            pltpu.VMEM((patches, 2 * capacity, LANES), F32),
            pltpu.VMEM((patches, 2 * capacity, LANES), F32),
            pltpu.VMEM((dets, 4 * modes_here, LANES), F32),
            pltpu.VMEM((dets, 4 * modes_here, LANES), F32),
            pltpu.VMEM((dets, 1, LANES), F32),
            pltpu.VMEM((dets, 1, LANES), F32),
            pltpu.VMEM((dets, 2 * rows, LANES), F32),
            pltpu.VMEM((dets, 2 * rows, LANES), F32),
            pltpu.VMEM((1, LANES), F32),
            pltpu.VMEM((dets, 1, LANES), F32),
            pltpu.VMEM((1, LANES), F32),
            pltpu.VMEM((patches, 1, LANES), F32),
            pltpu.SemaphoreType.DMA((INPUTS,)),
            pltpu.SemaphoreType.DMA((6,)),
            pltpu.SemaphoreType.DMA((6,)),
        ],
        compiler_params=pltpu.CompilerParams(
            collective_id=0, has_side_effects=True, vmem_limit_bytes=56 * 1024 * 1024
        ),
    )(*operands)
    new, pre, beta = pl.pallas_call(
        finish_kernel,
        out_shape=(
            jax.ShapeDtypeStruct(new.shape, F32),
            jax.ShapeDtypeStruct(pre.shape, F32),
            jax.ShapeDtypeStruct((1, 1), F32),
        ),
        in_specs=[vmem] * 3,
        out_specs=(vmem,) * 3,
        compiler_params=pltpu.CompilerParams(vmem_limit_bytes=1024 * 1024),
    )(new, pre, beta)
    return new.transpose(1, 0, 2)[None], pre.transpose(1, 0, 2)[None], beta.reshape(1)


def solution(mesh):
    placed = (
        P("patch", "det", None, None),
        P("patch", "det", None, None),
        P("patch", "det", None, None),
        P("patch", "det", None, None),
        P("patch", "det", None),
        P("patch", "det", None, None),
        P("patch", "det", None, None),
        P(),
        P("det", None, None),
        P("det", None),
    )
    return jax.shard_map(
        functools.partial(per_device, mesh.shape["patch"], mesh.shape["det"]),
        mesh=mesh,
        in_specs=placed,
        out_specs=(P("patch", "det", None, None), P("patch", "det", None, None), P()),
        check_vma=False,
    )
```

```python
import functools
import math

import jax
import jax.numpy as jnp
import numpy as np
from jax import lax
from jax.experimental import pallas as pl
from jax.experimental.pallas import tpu as pltpu
from jax.sharding import PartitionSpec as P

BF16 = jnp.bfloat16
F32 = jnp.float32
I32 = jnp.int32
MESH = pl.DeviceIdType.MESH
LANES = 128
RADIX = 8
GROUP = 16
HIGH = 4
LOW = 16
ROOT_HALF = math.sqrt(0.5)


def split2(x):
    hi = x.astype(BF16)
    return hi, (x - hi.astype(F32)).astype(BF16)


def split3(x):
    hi = x.astype(BF16)
    rest = x - hi.astype(F32)
    mid = rest.astype(BF16)
    return hi, mid, (rest - mid.astype(F32)).astype(BF16)


def dot(a, b):
    return lax.dot_general(a, b, (((1,), (0,)), ((), ())), preferred_element_type=F32)


def dot_nt(a, b):
    return lax.dot_general(a, b, (((1,), (1,)), ((), ())), preferred_element_type=F32)


def iota(shape, dim):
    return lax.broadcasted_iota(I32, shape, dim)


def stack_table(table):
    hi, lo = split2(table)
    return jnp.concatenate([hi, hi, lo], axis=0)


def fourier_matrix():
    j = np.arange(LANES)
    angle = 2.0 * np.pi * (np.outer(j, j) % LANES) / LANES
    c, s = np.cos(angle), np.sin(angle)
    return np.concatenate([c, s], axis=1).astype(np.float32)


def twiddle_rows():
    n = np.arange(LANES)
    angle = [2.0 * np.pi * n * k / (RADIX * LANES) for k in range(1, 5)]
    return np.stack([np.cos(a) for a in angle] + [np.sin(a) for a in angle]).astype(np.float32)


def cycle_matrix(modes_here):
    f = np.arange(256)[:, None]
    lane = np.arange(LANES)
    mode = (-(lane // modes_here) % (LANES // modes_here)) * modes_here + lane % modes_here
    angle = 2.0 * np.pi * (f * mode % 256) / 256.0
    scale = math.sqrt(2.0 / 256.0)
    return (np.concatenate([np.cos(angle), np.sin(angle)], axis=1) * scale).astype(np.float32)


def mode_rows(modes_here):
    row = np.arange(256)[:, None]
    owner, e, m = row // (2 * modes_here), row // modes_here % 2, row % modes_here
    mode = owner * modes_here + m
    angle = 2.0 * np.pi * (np.arange(256) * mode % 256) / 256.0
    rows = np.where(e == 0, np.cos(angle), np.sin(angle)) * math.sqrt(2.0 / 256.0)
    return rows.astype(np.float32)


def pixel_order():
    col = iota((1, 256), 1)
    s, pixel = col // 64, col % 64
    a, c = pixel // LOW, pixel % LOW
    source = jnp.where(s < 3, (c // 8) * LANES + (c % 8) * 16 + s * HIGH + a, -1)
    return (iota((256, 256), 0) == source).astype(F32).astype(BF16)


def double_angle(theta):
    n = jnp.round(theta * (2.0 / math.pi))
    odd = (n.astype(I32) & 1) == 1
    hi = np.float32(math.pi / 2)
    lo = np.float32(math.pi / 2 - float(hi))
    r = (theta - n * hi) - n * lo
    y = r * r
    c = jnp.full_like(y, COS_POLY[-1])
    for coef in COS_POLY[-2::-1]:
        c = c * y + coef
    s = jnp.full_like(y, SIN_POLY[-1])
    for coef in SIN_POLY[-2::-1]:
        s = s * y + coef
    return odd, c, s * r


def fit_polys():
    top = (math.pi / 4) ** 2 * 1.0001
    y = top * 0.5 * (1.0 - np.cos(np.pi * (np.arange(400) + 0.5) / 400))
    r = np.sqrt(y)
    power = y[:, None] ** np.arange(6)
    cos_c = np.linalg.lstsq(power, np.cos(2 * r), rcond=None)[0]
    sin_c = np.linalg.lstsq(power[:, :5], np.sin(2 * r) / r, rcond=None)[0]
    return [float(np.float32(v)) for v in cos_c], [float(np.float32(v)) for v in sin_c]


COS_POLY, SIN_POLY = fit_polys()


def noise_weights(own):
    col = iota((1, 5 * LANES), 1)
    k_of, j_of = col // LANES, col % LANES
    order = k_of + RADIX * j_of
    place = jnp.minimum(order, RADIX * LANES - order)
    pick = (iota((512, 5 * LANES), 0) == place).astype(F32).astype(BF16)
    dets = own.shape[0]
    parts = jnp.concatenate([part.astype(F32) for part in split3(own[:, :512])], axis=0)
    weight = dot(parts.astype(BF16), pick)
    weight = weight[:dets] + weight[dets : 2 * dets] + weight[2 * dets :]
    weight = weight + jnp.where(place == 512, own[:, 512:513], 0.0)
    edge = (k_of == 0) | (k_of == 4)
    return weight * jnp.where(edge, 1.0 / 1024.0, 2.0 / 1024.0)


def filter_blocks(x, weight, table, tw):
    blocks = x.shape[0]
    dets = weight.shape[0]
    t = [x[:, i * LANES : (i + 1) * LANES] for i in range(RADIX)]
    a = [t[i] + t[i + 4] for i in range(4)]
    b = [t[i] - t[i + 4] for i in range(4)]
    even, odd = a[0] + a[2], a[1] + a[3]
    diff, both = (b[1] - b[3]) * ROOT_HALF, (b[1] + b[3]) * ROOT_HALF
    y = [
        (even + odd, None),
        (b[0] + diff, -(b[2] + both)),
        (a[0] - a[2], a[3] - a[1]),
        (b[0] - diff, b[2] - both),
        (even - odd, None),
    ]
    rows = [jnp.concatenate([y[0][0], jnp.zeros_like(x[:, :LANES])], axis=1)]
    for k in range(1, 5):
        c, s = tw[k - 1 : k, :], tw[k + 3 : k + 4, :]
        re, im = y[k]
        if im is None:
            rows.append(jnp.concatenate([re * c, -(re * s)], axis=1))
        else:
            rows.append(jnp.concatenate([re * c + im * s, im * c - re * s], axis=1))
    hi, lo = split2(jnp.concatenate(rows, axis=0))
    spectrum = dot(jnp.concatenate([hi, lo, hi], axis=1), table)

    per = blocks // dets
    scaled = []
    for k in range(5):
        w = weight[:, k * LANES : (k + 1) * LANES]
        w = jnp.concatenate([w, -w], axis=1)
        for d in range(dets):
            part = spectrum[k * blocks + d * per : k * blocks + (d + 1) * per, :]
            scaled.append(part * w[d : d + 1, :])
    hi, lo = split2(jnp.concatenate(scaled, axis=0))
    u = dot(jnp.concatenate([hi, lo, hi], axis=1), table)
    re = [u[k * blocks : (k + 1) * blocks, :LANES] for k in range(5)]
    im = [u[k * blocks : (k + 1) * blocks, LANES:] for k in range(5)]
    tr, ti = [re[0]], [None]
    for k in range(1, 5):
        c, s = tw[k - 1 : k, :], tw[k + 3 : k + 4, :]
        tr.append(re[k] * c + im[k] * s)
        ti.append(re[k] * s - im[k] * c)
    plus, minus = tr[0] + tr[4], tr[0] - tr[4]
    p1, m1 = (tr[1] + ti[1]) * ROOT_HALF, (tr[1] - ti[1]) * ROOT_HALF
    p3, m3 = (tr[3] + ti[3]) * ROOT_HALF, (tr[3] - ti[3]) * ROOT_HALF
    e0, e1 = plus + tr[2], tr[1] + tr[3]
    f0, f1 = plus - tr[2], ti[3] - ti[1]
    g0, g1 = minus - ti[2], m1 - p3
    h0, h1 = minus + ti[2], m3 - p1
    return [e0 + e1, g0 + g1, f0 + f1, h0 + h1, e0 - e1, g0 - g1, f0 - f1, h0 - h1]


def bin_blocks(filtered, angle_ref, offset_ref, val_ref, low_ref, high_ref, binned_ref):
    blocks = angle_ref.shape[0]
    for i in range(RADIX):
        at = slice(i * LANES, (i + 1) * LANES)
        f = filtered[i]
        odd, c, s = double_angle(angle_ref[:, at])
        turned = jnp.where(odd, -f, f)
        for comp, v in enumerate((f, turned * c, turned * s)):
            hi, lo = split2(v)
            val_ref[comp, :, at] = hi
            val_ref[3 + comp, :, at] = lo
        off = offset_ref[:, at]
        low_ref[:, at] = (off & (LOW - 1)).astype(F32).astype(BF16)
        high_ref[:, at] = (off >> 4).astype(F32).astype(BF16)
    lane = iota((GROUP, LANES), 1) % 16

    def one_group(g, carry):
        rows = pl.ds(pl.multiple_of(g * GROUP, GROUP), GROUP)
        low, high = low_ref[rows, :], high_ref[rows, :]
        one, none = jnp.ones_like(low), jnp.zeros_like(low)
        ones = jnp.concatenate([jnp.where(low == k, one, none) for k in range(LOW)], axis=0)
        masks = [high == k for k in range(HIGH)]
        values = []
        for comp in range(6):
            v = val_ref[comp, rows, :]
            values += [jnp.where(masks[k], v, none) for k in range(HIGH)]
        got = dot_nt(jnp.concatenate(values, axis=0), ones)
        half = 3 * HIGH * GROUP
        got = got[:half, :] + got[half:, :]
        for h in range(2):
            acc = jnp.zeros((GROUP, LANES), F32)
            for sa in range(3 * HIGH):
                piece = got[sa * GROUP : (sa + 1) * GROUP, h * LANES : (h + 1) * LANES]
                moved = jnp.concatenate(
                    [
                        pltpu.roll(piece[:8], sa, 1, stride=15, stride_axis=0),
                        pltpu.roll(piece[8:], sa + 8, 1, stride=15, stride_axis=0),
                    ],
                    axis=0,
                )
                acc = jnp.where(lane == sa, moved, acc)
            binned_ref[rows, h * LANES : (h + 1) * LANES] = acc
        return carry

    lax.fori_loop(0, blocks // GROUP, one_group, 0, unroll=blocks // GROUP)
    turned = iota((blocks, LANES), 0)
    turned = turned + (turned >> 3 & 1)
    halves = []
    for h in range(2):
        part = binned_ref[:, h * LANES : (h + 1) * LANES]
        for bit in (1, 2, 4):
            part = jnp.where((turned & bit) != 0, pltpu.roll(part, LANES - 16 * bit, 1), part)
        halves.append(part)
    return jnp.concatenate(halves, axis=1)


def plan_route(patches, patch_row, block_row):
    blocks = patch_row.shape[1]
    capacity = 2 * blocks // patches
    quarter = capacity // 2
    patch_row = patch_row.astype(F32)
    block_row = block_row.astype(F32)
    patch_col = jnp.broadcast_to(patch_row, (blocks, blocks)).T
    same = patch_col == patch_row
    above = iota((blocks, blocks), 0)
    beside = iota((blocks, blocks), 1)
    slot_row = jnp.sum(jnp.where(same & (above < beside), 1.0, 0.0), axis=0, keepdims=True)
    slot_col = jnp.sum(jnp.where(same & (beside < above), 1.0, 0.0), axis=1, keepdims=True)
    place = patch_row * capacity + slot_row
    row = iota((2 * blocks, blocks), 0)
    own = row.astype(F32)
    first_half = row % capacity < quarter

    def choose(hit):
        return hit.astype(F32).astype(BF16)

    select = choose(own == place)
    select_a = choose((own == place) & first_half)
    select_b = choose((own + quarter == place) & first_half)
    named = jnp.where((row // capacity).astype(F32) == patch_row, block_row + 1.0, 0.0)
    slot_lane = (iota((blocks, LANES), 1) % capacity).astype(F32)
    labels = dot(named.astype(BF16), choose(slot_col == slot_lane))
    return (
        jnp.concatenate([select, select], axis=1),
        jnp.concatenate([select_a, select_a, select_b, select_b], axis=1),
        labels,
    )


def route(patches, binned, curvature, order, selects):
    front_select, back_select, labels = selects
    capacity = 2 * binned.shape[0] // patches
    hi, lo = split2(binned)
    moved = dot(jnp.concatenate([hi, lo], axis=1), jnp.concatenate([order, order], axis=0))
    hi, lo = split2(moved[:, :LANES])
    front = dot(front_select, jnp.concatenate([hi, lo], axis=0))
    back = moved[:, LANES:]
    hi, lo = split2(back)
    hi2, lo2 = split2(pltpu.roll(back, 64, 1))
    back = dot(back_select, jnp.concatenate([hi, lo, hi2, lo2], axis=0))
    labels = jnp.where(iota(labels.shape, 1) < 64, labels, curvature)
    back = jnp.where(iota(back.shape, 0) % capacity == capacity // 2, labels, back)
    return front, back


class Place:
    def __init__(self, patches, dets):
        self.tall, self.wide = patches // 4, dets // 4
        self.patch, self.det = lax.axis_index("patch"), lax.axis_index("det")
        self.y, corner = lax.div(self.patch, 4), lax.rem(self.patch, 4)
        far, core = lax.div(corner, 2), lax.rem(corner, 2)
        self.x, near = lax.div(self.det, 4), lax.rem(self.det, 4)
        across = self.x * 4 + lax.rem(near + 2, 4)
        self.patch_inner = [
            ((1 - far) * 2 + (1 - core), across),
            ((1 - far) * 2 + core, across),
            (far * 2 + (1 - core), self.det),
            (corner, self.det),
        ]
        self.det_inner = [lax.rem(near + step, 4) for step in (2, 1, 3, 0)]

    def each_patch(self, act):
        def lines(outer, count):
            turned = self.y + self.tall // 2 + (1 - 2 * lax.rem(outer, 2)) * lax.div(outer + 1, 2)
            base = lax.rem(turned, self.tall) * 4
            for corner, det in self.patch_inner[:count]:
                act(base + corner, det, base + corner)

        self.walk(self.tall, lines)

    def each_det(self, act):
        def lines(outer, count):
            turned = self.x + self.wide // 2 + (1 - 2 * lax.rem(outer, 2)) * lax.div(outer + 1, 2)
            base = lax.rem(turned, self.wide) * 4
            for near in self.det_inner[:count]:
                act(self.patch, base + near, base + near)

        self.walk(self.wide, lines)

    def walk(self, count, lines):
        def one(outer, carry):
            lines(outer, 4)
            return carry

        lax.fori_loop(0, count - 1, one, 0)
        lines(jnp.int32(count - 1), 3)


def start_exchange(each, me, send_at, recv_at, send_sem, recv_sem):
    def act(patch, det, index):
        pltpu.make_async_remote_copy(
            src_ref=send_at(index),
            dst_ref=recv_at(me),
            send_sem=send_sem,
            recv_sem=recv_sem,
            device_id=(patch, det),
            device_id_type=MESH,
        ).start()

    each(act)
    pltpu.make_async_copy(send_at(me), recv_at(me), recv_sem).start()


def await_bytes(ref, sem):
    pltpu.make_async_copy(ref, ref, sem).wait()


def fold_rows(x, step):
    wrapped = pltpu.roll(pltpu.roll(x, x.shape[0] - step, 0), 64, 1)
    return jnp.where(iota(x.shape, 1) < 64, x, wrapped)


def legendre_columns(columns, legendre, modes_here):
    hi, lo = split2(columns)
    leg_hi, leg_lo = legendre
    product = dot_nt(hi, leg_hi) + dot_nt(lo, leg_hi) + dot_nt(hi, leg_lo)
    rows = 6 * modes_here
    mode_of = iota((rows, 64), 0) % modes_here
    coef = jnp.zeros((rows, 64), F32)
    for m in range(modes_here):
        coef = jnp.where(mode_of == m, product[:rows, m * 64 : (m + 1) * 64], coef)
    return coef


def step_kernel(patches, dets, *refs):
    hbm, refs = refs[:INPUTS], refs[INPUTS:]
    (new_ref, pre_ref, beta_ref), refs = refs[:3], refs[3:]
    held, refs = refs[:INPUTS], refs[INPUTS:]
    (
        val_ref, low_ref, high_ref, binned_ref,
        send1, recv1, send2, recv2, send3, recv3, send_map, recv_map, send4, recv4, send5, recv5,
        in_sems, send_sems, recv_sems,
    ) = refs
    place = Place(patches, dets)
    over_patch = (place.each_patch, place.patch)
    over_det = (place.each_det, place.det)
    fetches = [
        pltpu.make_async_copy(src, dst, in_sems.at[i]) for i, (src, dst) in enumerate(zip(hbm, held))
    ]
    for fetch in fetches[:FIRST]:
        fetch.start()
    barrier = pltpu.get_barrier_semaphore()

    def greet(patch, det, index):
        pl.semaphore_signal(barrier, inc=1, device_id=(patch, det), device_id_type=MESH)

    place.each_patch(greet)
    place.each_det(greet)
    (
        x_ref, table_ref, tw_ref, spec_ref, patch_ref, block_ref, angle_ref, offset_ref,
        res_ref, cycle_ref, modes_ref, leg_ref, filt_ref, rz_ref,
    ) = held

    for fetch in fetches[3:6]:
        fetch.wait()
    selects = plan_route(patches, patch_ref[...], block_ref[...])
    order = pixel_order()
    weight = noise_weights(spec_ref[...])
    for fetch in fetches[FIRST : FIRST + 2]:
        fetch.start()
    for fetch in fetches[:3]:
        fetch.wait()
    x = x_ref[...]
    waves = table_ref[...]
    swapped = jnp.concatenate([waves[:, LANES:], waves[:, :LANES]], axis=1)
    signed = jnp.where(iota(waves.shape, 1) < LANES, waves, -waves)
    table = stack_table(jnp.concatenate([signed, swapped], axis=0))
    filtered = filter_blocks(x, weight, table, tw_ref[...])
    total = jnp.zeros((x.shape[0], LANES), F32)
    for i in range(RADIX):
        total = total + x[:, i * LANES : (i + 1) * LANES] * filtered[i]
    curvature = jnp.sum(jnp.sum(total, axis=0, keepdims=True), axis=1, keepdims=True)
    for fetch in fetches[FIRST : FIRST + 2]:
        fetch.wait()
    for fetch in fetches[FIRST + 2 :]:
        fetch.start()
    binned = bin_blocks(filtered, angle_ref, offset_ref, val_ref, low_ref, high_ref, binned_ref)
    front, back = route(patches, binned, curvature, order, selects)
    def drain(count, ref, index):
        await_bytes(ref.at[pl.ds(0, count - 1)], send_sems.at[index])

    capacity = front.shape[0] // patches
    half = capacity // 2
    send1[:, :capacity, :] = front.reshape(patches, capacity, LANES)
    send1[:, capacity:, :] = back.reshape(patches, capacity, LANES)
    pl.semaphore_wait(barrier, patches + dets - 2)
    used1 = capacity + half + 1
    start_exchange(
        *over_patch,
        lambda p: send1.at[p, pl.ds(0, used1)], lambda p: recv1.at[p, pl.ds(0, used1)],
        send_sems.at[0], recv_sems.at[0],
    )

    for fetch in fetches[FIRST + 2 :]:
        fetch.wait()
    rows = res_ref.shape[1]
    modes_here = LANES // dets
    lines = []
    for s in range(3):
        old = res_ref[s]
        for ring in range(rows // 4):
            lines.append(
                jnp.concatenate([old[ring * 4 + q : ring * 4 + q + 1, :] for q in range(4)], axis=1)
            )
    lines.append(jnp.zeros((8 - len(lines), 256), F32))
    hi, lo = split2(jnp.concatenate(lines, axis=0))
    modes = dot(jnp.concatenate([hi, lo, hi], axis=1), stack_table(cycle_ref[...]))
    slot = iota((dets, LANES), 1) // modes_here
    message = jnp.zeros((dets, LANES), F32)
    for s in range(3):
        for ring in range(rows // 4):
            at = s * (rows // 4) + ring
            for e in range(2):
                target = ring * 16 + 2 * s + e
                line = modes[at : at + 1, e * LANES : (e + 1) * LANES]
                moved = pltpu.roll(
                    jnp.broadcast_to(line, (dets, LANES)), 0, 1, stride=modes_here, stride_axis=0
                )
                moved = pltpu.roll(moved, target * modes_here, 1)
                message = jnp.where(slot == target, moved, message)
    for d in range(dets):
        send3[d] = message[d : d + 1, :]
    start_exchange(
        *over_det, lambda d: send3.at[d], lambda d: recv3.at[d],
        send_sems.at[2], recv_sems.at[2],
    )

    mode_hi, mode_lo = split2(modes_ref[...])
    mode_table = jnp.concatenate([mode_hi, mode_lo, mode_hi], axis=1)
    row = iota((256, patches * capacity), 0)
    interleaved = (row % 64 * 4 + row // 64 + 1).astype(F32)
    await_bytes(recv1.at[:, pl.ds(0, used1)], recv_sems.at[0])
    got0 = recv1[:, :capacity, :].reshape(patches * capacity, LANES)
    got1 = recv1[:, capacity:, :]
    tags = jnp.sum(jnp.where(iota(got1.shape, 1) == half, got1, 0.0), axis=1)
    got1 = jnp.where(iota(got1.shape, 1) < half, got1, 0.0).reshape(patches * capacity, LANES)
    curve = jnp.sum(tags, axis=0, keepdims=True)
    tags = jnp.where(iota(tags.shape, 1) < 64, tags, pltpu.roll(tags, 64, 1))
    per = LANES // capacity
    labels = jnp.concatenate(
        [
            jnp.sum(
                jnp.where(iota(tags.shape, 1) // capacity + h * per == iota(tags.shape, 0), tags, 0.0),
                axis=0,
                keepdims=True,
            )
            for h in range(patches // per)
        ],
        axis=1,
    )
    labels_b = pltpu.roll(labels, labels.shape[1] - half, 1)
    hi, lo = split2(got0)
    rhs0 = jnp.concatenate([hi, lo], axis=0)
    hi, lo = split2(got1)
    hi2, lo2 = split2(pltpu.roll(got1, 64, 1))
    rhs1 = jnp.concatenate([hi, lo, hi2, lo2], axis=0)

    def spread(target):
        hit = (target == labels).astype(F32).astype(BF16)
        hit_b = (target == labels_b).astype(F32).astype(BF16)
        return (
            dot(jnp.concatenate([hit, hit], axis=1), rhs0),
            dot(jnp.concatenate([hit, hit, hit_b, hit_b], axis=1), rhs1),
        )

    map0, map1 = spread(interleaved)
    left = iota((64, LANES), 1) < 64
    fields = []
    for s in range(3):
        source = map1 if s == 2 else map0
        tiles = []
        for h in range(2):
            a = source[h * 128 : h * 128 + 64, :]
            b = source[h * 128 + 64 : h * 128 + 128, :]
            if s == 1:
                tiles.append(jnp.where(left, pltpu.roll(a, 64, 1), b))
            else:
                tiles.append(jnp.where(left, a, pltpu.roll(b, 64, 1)))
        fields.append(jnp.concatenate(tiles, axis=1))
    hi, lo = split2(jnp.concatenate(fields, axis=0))
    modes = dot_nt(
        mode_table,
        jnp.concatenate([hi, hi, lo], axis=1),
    )
    group = 2 * modes_here
    modes1 = fold_rows(
        jnp.concatenate([modes[:, LANES:], jnp.zeros((256, 64), F32)], axis=1), modes_here
    )
    modes1 = jnp.where(iota(modes1.shape, 0) % group == modes_here, curve, modes1)
    send2[:, :group, :] = modes[:, :LANES].reshape(dets, group, LANES)
    send2[:, group:, :] = modes1.reshape(dets, group, LANES)
    used2 = group + modes_here + 1
    start_exchange(
        *over_det,
        lambda d: send2.at[d, pl.ds(0, used2)], lambda d: recv2.at[d, pl.ds(0, used2)],
        send_sems.at[1], recv_sems.at[1],
    )

    map0, map1 = spread((row + 1).astype(F32))
    used_map = rows + rows // 2
    send_map[:, :rows, :] = map0.reshape(dets, rows, LANES)
    send_map[:, rows:, :] = fold_rows(map1, rows // 2).reshape(dets, rows, LANES)
    await_bytes(recv3, recv_sems.at[2])
    cycles = recv3[...].reshape(dets, LANES)
    cycles = jnp.concatenate([cycles, pltpu.roll(cycles, 64, 1)], axis=0)
    cycles = jnp.concatenate([cycles, jnp.zeros((LANES - 2 * dets, LANES), F32)], axis=0).T
    columns = 6 * modes_here
    ring_of = iota((2 * dets, 2 * dets), 0)
    column = iota((2 * dets, 2 * dets), 1)
    order = (ring_of == 2 * (column % dets) + column // dets).astype(F32).astype(BF16)
    legendre = leg_ref[...].reshape(modes_here * 64, 2 * dets)
    a, b, c = split3(legendre)
    coef_old = legendre_columns(
        cycles[: columns + 8, : 2 * dets],
        split2(dot(a, order) + dot(b, order) + dot(c, order)),
        modes_here,
    )
    legendre = split2(legendre)
    weight = jnp.concatenate([filt_ref[...]] * 6, axis=0)
    rz_before = rz_ref[0]

    await_bytes(recv2.at[:, pl.ds(0, used2)], recv_sems.at[1])
    sum0 = jnp.sum(recv2[:, :group, :], axis=0)
    sum1 = jnp.sum(recv2[:, group:, :], axis=0)
    step_size = rz_before / sum1[modes_here : modes_here + 1, 64:65]
    turned0, turned1 = pltpu.roll(sum0, 64, 1), pltpu.roll(sum1, 64, 1)
    image_modes = jnp.concatenate(
        [sum0, turned0, sum1[:modes_here], turned1[:modes_here], jnp.zeros((8, LANES), F32)], axis=0
    )[:, :64]
    coef = coef_old - step_size * legendre_columns(image_modes, legendre, modes_here)
    pre = weight * coef
    rz = jnp.sum(jnp.sum(pre * coef, axis=0, keepdims=True), axis=1, keepdims=True)
    send4[...] = jnp.broadcast_to(rz, (1, LANES))
    start_exchange(
        *over_det, lambda d: send4, lambda d: recv4.at[d], send_sems.at[3], recv_sems.at[3]
    )
    drain(dets, recv2.at[:, pl.ds(0, used2)], 1)
    start_exchange(
        *over_det,
        lambda d: send_map.at[d, pl.ds(0, used_map)], lambda d: recv_map.at[d, pl.ds(0, used_map)],
        send_sems.at[5], recv_sems.at[5],
    )
    for c in range(6):
        pre_ref[c] = pre[c * modes_here : (c + 1) * modes_here, :]

    await_bytes(recv4, recv_sems.at[3])
    send5[...] = jnp.sum(recv4[...], axis=0)
    start_exchange(
        *over_patch, lambda p: send5, lambda p: recv5.at[p],
        send_sems.at[4], recv_sems.at[4],
    )
    await_bytes(recv_map.at[:, pl.ds(0, used_map)], recv_sems.at[5])
    image0 = jnp.sum(recv_map[:, :rows, :], axis=0)
    image1 = jnp.sum(recv_map[:, rows:, :], axis=0)
    low = rows // 2
    image1 = jnp.concatenate([image1[:low], pltpu.roll(image1, 64, 1)[:low]], axis=0)
    new_ref[0] = res_ref[0] - step_size * image0[:, :64]
    new_ref[1] = res_ref[1] - step_size * pltpu.roll(image0, 64, 1)[:, :64]
    new_ref[2] = res_ref[2] - step_size * image1[:, :64]

    await_bytes(recv5, recv_sems.at[4])
    beta_ref[...] = jnp.sum(recv5[...], axis=0) / rz_before

    drain(patches, recv1.at[:, pl.ds(0, used1)], 0)
    drain(dets, recv3, 2)
    drain(dets, recv4, 3)
    drain(patches, recv5, 4)
    drain(dets, recv_map.at[:, pl.ds(0, used_map)], 5)


def finish_kernel(new_in, pre_in, beta_in, new_ref, pre_ref, beta_ref):
    new_ref[...] = new_in[...]
    pre_ref[...] = pre_in[...]
    beta_ref[...] = beta_in[:, :1]


INPUTS = 14
FIRST = 6


def per_device(
    patches, dets, tod_image, angles, pixel_offset, target_patch, target_block, noise_spectrum,
    residual, previous_rz, legendre, harmonic_filter,
):
    blocks, length = tod_image.shape[2:]
    vmem = pl.BlockSpec(memory_space=pltpu.VMEM)
    hbm = pl.BlockSpec(memory_space=pl.ANY)
    capacity = 2 * blocks // patches
    rows = residual.shape[1]
    modes_here = legendre.shape[0]
    operands = (
        tod_image[0, 0],
        jnp.asarray(fourier_matrix()),
        jnp.asarray(twiddle_rows()),
        noise_spectrum[0, 0],
        target_patch.reshape(1, blocks),
        target_block.reshape(1, blocks),
        angles[0, 0],
        pixel_offset[0, 0],
        residual[0].transpose(1, 0, 2),
        jnp.asarray(cycle_matrix(modes_here)),
        jnp.asarray(mode_rows(modes_here)),
        legendre,
        harmonic_filter,
        previous_rz,
    )
    new, pre, beta = pl.pallas_call(
        functools.partial(step_kernel, patches, dets),
        out_shape=(
            pltpu.VMEM((3, rows, 64), F32),
            pltpu.VMEM((6, modes_here, 64), F32),
            pltpu.VMEM((1, LANES), F32),
        ),
        in_specs=[hbm] * INPUTS,
        out_specs=(vmem, vmem, vmem),
        scratch_shapes=[pltpu.VMEM(a.shape, a.dtype) for a in operands[:-1]]
        + [pltpu.SMEM((1,), F32)]
        + [
            pltpu.VMEM((6, blocks, length), BF16),
            pltpu.VMEM((blocks, length), BF16),
            pltpu.VMEM((blocks, length), BF16),
            pltpu.VMEM((blocks, 256), F32),
            pltpu.VMEM((patches, 2 * capacity, LANES), F32),
            pltpu.VMEM((patches, 2 * capacity, LANES), F32),
            pltpu.VMEM((dets, 4 * modes_here, LANES), F32),
            pltpu.VMEM((dets, 4 * modes_here, LANES), F32),
            pltpu.VMEM((dets, 1, LANES), F32),
            pltpu.VMEM((dets, 1, LANES), F32),
            pltpu.VMEM((dets, 2 * rows, LANES), F32),
            pltpu.VMEM((dets, 2 * rows, LANES), F32),
            pltpu.VMEM((1, LANES), F32),
            pltpu.VMEM((dets, 1, LANES), F32),
            pltpu.VMEM((1, LANES), F32),
            pltpu.VMEM((patches, 1, LANES), F32),
            pltpu.SemaphoreType.DMA((INPUTS,)),
            pltpu.SemaphoreType.DMA((6,)),
            pltpu.SemaphoreType.DMA((6,)),
        ],
        compiler_params=pltpu.CompilerParams(
            collective_id=0, has_side_effects=True, vmem_limit_bytes=56 * 1024 * 1024
        ),
    )(*operands)
    new, pre, beta = pl.pallas_call(
        finish_kernel,
        out_shape=(
            jax.ShapeDtypeStruct(new.shape, F32),
            jax.ShapeDtypeStruct(pre.shape, F32),
            jax.ShapeDtypeStruct((1, 1), F32),
        ),
        in_specs=[vmem] * 3,
        out_specs=(vmem,) * 3,
        compiler_params=pltpu.CompilerParams(vmem_limit_bytes=1024 * 1024),
    )(new, pre, beta)
    return new.transpose(1, 0, 2)[None], pre.transpose(1, 0, 2)[None], beta.reshape(1)


def solution(mesh):
    placed = (
        P("patch", "det", None, None),
        P("patch", "det", None, None),
        P("patch", "det", None, None),
        P("patch", "det", None, None),
        P("patch", "det", None),
        P("patch", "det", None, None),
        P("patch", "det", None, None),
        P(),
        P("det", None, None),
        P("det", None),
    )
    return jax.shard_map(
        functools.partial(per_device, mesh.shape["patch"], mesh.shape["det"]),
        mesh=mesh,
        in_specs=placed,
        out_specs=(P("patch", "det", None, None), P("patch", "det", None, None), P()),
        check_vma=False,
    )
```
